256 devices in a mesh: layer: 64 (over z, x, core), dp: 4 (over y).
Axes of the slice: x: 4, y: 4, z: 8, core: 2. Of those that a mesh axis runs over, the one named last changes fastest.
Arguments:
- states: bfloat16 [128, 4, 16, 16, 256], P('layer', 'dp'), may hold values from -6 to 6
- kernels: bfloat16 [128, 3, 3, 256, 256], P('layer'), may hold values from -0.125 to 0.125
- adjoint_guess: float32 [64, 4, 16, 16, 256], P('layer', 'dp'), may hold values from -6 to 6
- coarse_gain: float32 [64, 16, 16, 256], P('layer'), may hold values from 0 to 1, as said below
- terminal: float32 [4, 16, 16, 256], P('dp'), may hold values from -6 to 6
Outputs:
- adjoint: float32 [128, 4, 16, 16, 256], P('layer', 'dp')
- weight_grad: float32 [128, 3, 3, 256, 256], P('layer', None, None, None, 'dp')
The draws below stay inside these ranges and needn't reach their ends.
Inputs may be any that keep to these rules, and one draw needn't show every extreme that they name: `coarse_gain`: strictly positive.
All inputs are finite; a program needn't handle non-finite values.
Results may differ from the reference program's by a relative error of at most 0.015.
Values may be sent and summed in bfloat16 or wider, within the bound.
No kernel may reach another device: no remote copies, remote signals or barrier semaphores. Data moves between devices by JAX's collectives and lax.ppermute only.
A program may use at most 128 MiB of HBM per device.

```python
import math
import jax
import jax.numpy as jnp
from jax import lax

C = 256
H = 16
W = 16
SLAB_COUNT = 64
NL = 128
B = 4


def draw_coarse_gain(key, part):
    key = jax.random.fold_in(key, 7)
    rate_random_key, jitter_random_key, spike_random_key = jax.random.split(key, 3)
    logarithm_rate = jax.random.uniform(rate_random_key, (C,), jnp.float32, math.log(0.3), math.log(200.0))
    jitter_noise = jax.random.uniform(jitter_random_key, (SLAB_COUNT, H, W, C), jnp.float32, 0.5, 1.5)
    spike_sample = jax.random.uniform(spike_random_key, (SLAB_COUNT, 1, 1, 1), jnp.float32, 0.0, 1.0)
    spike_factor = jnp.where(spike_sample < 0.06, 0.6, 1.0)
    coupling_gain = jnp.exp(-jnp.exp(logarithm_rate) * jitter_noise / SLAB_COUNT) * spike_factor
    return coupling_gain.astype(jnp.float32)


def block_levels(rng, dims, cuts, least, largest):
    gain = 1.0
    for position, blocks in cuts:
        heights = jax.random.uniform(jax.random.fold_in(jax.random.fold_in(rng, 6), position), (blocks,), jnp.float32, least / len(cuts), largest / len(cuts))
        gain = gain * jnp.repeat(jnp.exp(heights), dims[position] // blocks).reshape((-1,) + (1,) * (len(dims) - 1 - position))
    return gain


def gaussian(rng, extent, scale, most, shards=(), dtype=jnp.bfloat16):
    result = jax.random.normal(rng, extent, jnp.float32) * scale
    if len(shards) > 0:
        result = block_levels(rng, extent, shards, -0.22, 0.18) * result
    return jnp.clip(result, min=-most, max=most).astype(dtype)


def setup_inputs(seed: int = 0) -> dict:
    seeds = jax.random.split(jax.random.key(seed), 6)
    states = gaussian(seeds[0], (NL, B, H, W, C), 1.0, 6.0, ((0, 64), (1, 4)))
    kernels = gaussian(seeds[1], (NL, 3, 3, C, C), (9 * C) ** -0.5, 0.125, ((0, 64),))
    adjoint_guess = gaussian(seeds[2], (SLAB_COUNT, B, H, W, C), 1.0, 6.0, ((0, 64), (1, 4)), jnp.float32)
    coarse_gain = draw_coarse_gain(jax.random.fold_in(seeds[5], 71), 0)
    terminal = gaussian(seeds[4], (B, H, W, C), 1.0, 6.0, ((0, 4),), jnp.float32)
    return dict(states=states, kernels=kernels, adjoint_guess=adjoint_guess, coarse_gain=coarse_gain, terminal=terminal)


STEP = 0.5
DAMPING = 0.5


def forward_conv(layer_state, kernel):
    return lax.conv_general_dilated(layer_state, kernel, (1, 1), "SAME", dimension_numbers=("NHWC", "HWIO", "NHWC"), preferred_element_type=jnp.float32)


def adjoint_conv(signal, kernel):
    return lax.conv_general_dilated(signal, kernel[::-1, ::-1], (1, 1), "SAME", dimension_numbers=("NHWC", "HWOI", "NHWC"), preferred_element_type=jnp.float32)


def sensitivity(layer_state, kernel):
    activation = jnp.tanh(forward_conv(layer_state, kernel))
    return 1.0 - activation * activation


def adjoint_step(carried, slopes, kernel):
    signal = (slopes * carried).astype(jnp.bfloat16)
    return carried + STEP * adjoint_conv(signal, kernel)


def relax(right_value, slopes, kernels, lowest):
    values = []
    carried = right_value
    for block_index in range(slopes.shape[0] - 1, lowest - 1, -1):
        carried = adjoint_step(carried, slopes[block_index], kernels[block_index])
        values.append(carried)
    return jnp.stack(values[::-1])


def tap_products(layer_state, signal):
    height = layer_state.shape[1]
    width = layer_state.shape[2]
    channels = layer_state.shape[3]
    padded = jnp.pad(layer_state, ((0, 0), (1, 1), (1, 1), (0, 0)))
    signal_rows = signal.reshape(-1, signal.shape[-1])
    tap_list = []
    for row_tap in range(3):
        for col_tap in range(3):
            patch_rows = padded[:, row_tap:row_tap + height, col_tap:col_tap + width, :].reshape(-1, channels)
            tap_list.append(lax.dot_general(patch_rows, signal_rows, (((0,), (0,)), ((), ())), preferred_element_type=jnp.float32))
    return jnp.stack(tap_list).reshape(3, 3, channels, signal_rows.shape[-1])


def reference(states, kernels, adjoint_guess, coarse_gain, terminal):
    slabs = coarse_gain.shape[0]
    total_depth = kernels.shape[0]
    per_slab = total_depth // slabs
    slab_states = states.reshape((slabs, per_slab) + states.shape[1:])
    slab_kernels = kernels.reshape((slabs, per_slab) + kernels.shape[1:])
    slopes = jax.vmap(jax.vmap(sensitivity))(slab_states, slab_kernels)
    last_value = terminal.astype(jnp.float32)

    def shifted(points):
        return jnp.concatenate([points[1:], last_value[None]], 0)

    sweep = jax.vmap(lambda right_value, slope_set, kernel_set: relax(right_value, slope_set, kernel_set, 0)[0])
    points = adjoint_guess.astype(jnp.float32)
    for sweep_index in range(2):
        points = points + DAMPING * (sweep(shifted(points), slopes, slab_kernels) - points)
    neighbours = shifted(points)
    residual = sweep(neighbours, slopes, slab_kernels) - points

    def backward(carry, item):
        coupling_gain, term = item
        error = coupling_gain[None] * carry + term
        return error, error

    unused, errors = lax.scan(backward, jnp.zeros_like(points[0]), (coarse_gain, residual), reverse=True)
    corrected = points + errors
    rights = shifted(corrected)
    inner_points = jax.vmap(lambda right_value, slope_set, kernel_set: relax(right_value, slope_set, kernel_set, 1))(rights, slopes, slab_kernels)
    adjoint = jnp.concatenate([corrected[:, None], inner_points], 1)
    following = jnp.concatenate([adjoint[:, 1:], rights[:, None]], 1)
    signals = (slopes * following).astype(jnp.bfloat16)
    flat_signals = signals.reshape((total_depth,) + states.shape[1:])
    grads = lax.map(lambda pair: tap_products(pair[0], pair[1]), (states, flat_signals))
    return adjoint.reshape(states.shape), STEP * grads
```

```python
import functools

import jax
import jax.numpy as jnp
from jax import lax
from jax.experimental import pallas as pl
from jax.experimental.pallas import tpu as pltpu
from jax.sharding import PartitionSpec as P

STEP = 0.5
DAMPING = 0.5
BF = jnp.bfloat16
F32 = jnp.float32
VMEM_LIMIT = 24 * 1024 * 1024


def call(body, outs, n_in, smem=(), flops=0, name=None):
    return pl.pallas_call(
        body,
        out_shape=outs,
        in_specs=[
            pl.BlockSpec(memory_space=pltpu.SMEM if k in smem else pltpu.VMEM)
            for k in range(n_in)
        ],
        out_specs=jax.tree.map(lambda _: pl.BlockSpec(memory_space=pltpu.VMEM), outs),
        compiler_params=pltpu.CompilerParams(vmem_limit_bytes=VMEM_LIMIT),
        cost_estimate=pl.CostEstimate(flops=flops, bytes_accessed=2_000_000, transcendentals=0),
        name=name,
    )


def columns(value, width):
    cells = value.shape[0]
    col = lax.broadcasted_iota(jnp.int32, value.shape, 0) % width
    ahead = jnp.where(col == width - 1, 0.0, pltpu.roll(value, cells - 1, 0))
    behind = jnp.where(col == 0, 0.0, pltpu.roll(value, 1, 0))
    return ahead, value, behind


def rows(value, width):
    edge = jnp.zeros((width, value.shape[1]), value.dtype)
    return jnp.concatenate([edge, value, edge], 0)


def forward_patches(value, width):
    cells = value.shape[0]
    ahead, here, behind = columns(value, width)
    padded = [rows(part.astype(BF), width) for part in (behind, here, ahead)]
    return [padded[j][i * width : i * width + cells] for i in range(3) for j in range(3)]


def adjoint_patches(value, width):
    cells = value.shape[0]
    ahead, here, behind = columns(value, width)
    padded = [rows(part.astype(BF), width) for part in (ahead, here, behind)]
    return [padded[j][(2 - i) * width : (2 - i) * width + cells] for i in range(3) for j in range(3)]


def adjoint_conv(signal, turned_ref, block, width):
    patches = jnp.concatenate(adjoint_patches(signal, width), 1)
    return jnp.dot(patches, turned_ref[block], preferred_element_type=F32)


def block_map(value, slope, turned_ref, block, width):
    signal = (slope * value).astype(BF).astype(F32)
    return value + STEP * adjoint_conv(signal, turned_ref, block, width)


def relaxed(right, slope_ref, turned_ref, width):
    for block in range(slope_ref.shape[0] - 1, -1, -1):
        right = block_map(right, slope_ref[block], turned_ref, block, width)
    return right


def slope_body(width, states_ref, kernels_ref, slope_ref, turned_ref):
    blocks, _, height, _, channels = states_ref.shape
    for block in range(blocks):
        value = states_ref[block, 0].reshape(height * width, channels).astype(F32)
        patches = jnp.concatenate(forward_patches(value, width), 1)
        taps = kernels_ref[block].reshape(9 * channels, channels)
        act = jnp.tanh(jnp.dot(patches, taps, preferred_element_type=F32))
        slope_ref[block] = 1.0 - act * act
        for i in range(3):
            for j in range(3):
                at = (i * 3 + j) * channels
                turned_ref[block, at : at + channels, :] = kernels_ref[block, i, j].T


def entering(flag_ref, arriving_ref, terminal_ref):
    return jnp.where(flag_ref[0] == 1, terminal_ref[...], arriving_ref[...].astype(F32))


def sweep_body(width, flag_ref, arriving_ref, terminal_ref, points_ref, slope_ref, turned_ref, out_ref, send_ref):
    right = entering(flag_ref, arriving_ref, terminal_ref)
    points = points_ref[...]
    points = points + DAMPING * (relaxed(right, slope_ref, turned_ref, width) - points)
    out_ref[...] = points
    send_ref[...] = points.astype(BF)


def residual_body(width, flag_ref, arriving_ref, terminal_ref, points_ref, slope_ref, turned_ref, gain_ref, relax_ref, send_ref):
    right = entering(flag_ref, arriving_ref, terminal_ref)
    relax = relaxed(right, slope_ref, turned_ref, width)
    relax_ref[...] = relax
    residual = (relax - points_ref[...]).reshape(32, 8, 256)
    decay = (1.0 - gain_ref[...]).reshape(32, 8, 256)
    for half in range(2):
        lanes = slice(128 * half, 128 * half + 128)
        send_ref[:, half] = jnp.concatenate([residual[:, :, lanes], decay[:, :, lanes]], 1).astype(BF)


def scan_body(given_ref, out_ref):
    count = given_ref.shape[0]
    error = jnp.zeros((8, 128), F32)
    for at in range(count - 1, -1, -1):
        out_ref[at] = error.astype(BF)
        term = given_ref[at].astype(F32)
        error = error - term[8:] * error + term[:8]


def final_body(width, flag_ref, arriving_ref, terminal_ref, error_ref, gain_ref, relax_ref, slope_ref, turned_ref, adjoint_ref, signal_ref):
    error = error_ref[...].astype(F32).reshape(32, 2, 8, 128)
    error = jnp.concatenate([error[:, 0], error[:, 1]], 2).reshape(256, 256)
    right = entering(flag_ref, arriving_ref, terminal_ref) + error
    adjoint_ref[0] = gain_ref[...] * error + relax_ref[...]
    slope = slope_ref[1]
    last = (slope * right).astype(BF).astype(F32)
    inner = right + STEP * adjoint_conv(last, turned_ref, 1, width)
    adjoint_ref[1] = inner
    first = (slope_ref[0] * inner).astype(BF).astype(F32)
    low = lax.broadcasted_iota(jnp.int32, (128, 128), 1) < 64
    for block, signal in ((0, first), (1, last)):
        for half in range(2):
            top = signal[:128, 128 * half : 128 * half + 128]
            bottom = signal[128:, 128 * half : 128 * half + 128]
            signal_ref[2 * half, block] = jnp.where(low, top, pltpu.roll(bottom, 64, 1)).astype(BF)
            signal_ref[2 * half + 1, block] = jnp.where(low, pltpu.roll(top, 64, 1), bottom).astype(BF)


def turn_body(states_ref, out_ref):
    images, blocks = states_ref.shape[:2]
    for block in range(blocks):
        for image in range(images):
            out_ref[block, :, 256 * image : 256 * image + 256] = states_ref[image, block].T


def taps_body(width, images, *refs):
    states_ref, signal_refs, out_ref = refs[0], refs[1 : 1 + images], refs[1 + images]
    low = lax.broadcasted_iota(jnp.int32, (128, 128), 1) < 64
    wide = lax.broadcasted_iota(jnp.int32, (256, 128), 1) < 64
    for block in range(out_ref.shape[0]):
        parts = []
        for image in range(images):
            packed = signal_refs[image][block].astype(F32)
            other = pltpu.roll(packed, 64, 1)
            both = jnp.concatenate([jnp.where(low, packed, other), jnp.where(low, other, packed)], 0)
            patches = adjoint_patches(both, width)
            patches.append(patches[-1])
            parts.append(
                jnp.concatenate([jnp.where(wide, patches[2 * k], patches[2 * k + 1]) for k in range(5)], 1)
            )
        moved = jnp.concatenate(parts, 0)
        grads = STEP * jnp.dot(states_ref[block], moved, preferred_element_type=F32)
        for tap in range(9):
            out_ref[block, tap // 3, tap % 3] = grads[:, 64 * tap : 64 * tap + 64]


def on_device(states, kernels, adjoint_guess, coarse_gain, terminal):
    blocks, _, height, width, channels = states.shape
    cells = height * width
    slabs = lax.axis_size("layer")
    images = lax.axis_size("dp")
    here = lax.axis_index("dp")
    flag = (lax.axis_index("layer") == slabs - 1).astype(jnp.int32).reshape(1)
    conv_flops = 2 * cells * 9 * channels * channels
    shape = jax.ShapeDtypeStruct

    def from_right(points):
        return lax.ppermute(points, "layer", [((i + 1) % slabs, i) for i in range(slabs)])

    points = adjoint_guess.reshape(cells, channels)
    last_value = terminal.reshape(cells, channels)
    gain = coarse_gain.reshape(cells, channels)
    arriving = from_right(points.astype(BF))
    gathered = lax.all_gather(states.reshape(blocks, cells, channels), "dp")
    slopes, turned = call(
        functools.partial(slope_body, width),
        (shape((blocks, cells, channels), F32), shape((blocks, 9 * channels, channels), BF)),
        2,
        flops=blocks * conv_flops,
        name="slopes",
    )(states, kernels)
    for sweep_index in range(2):
        points, send = call(
            functools.partial(sweep_body, width),
            (shape((cells, channels), F32), shape((cells, channels), BF)),
            6,
            smem=(0,),
            flops=blocks * conv_flops,
            name="sweep",
        )(flag, arriving, last_value, points, slopes, turned)
        arriving = from_right(send)
    relax, send = call(
        functools.partial(residual_body, width),
        (shape((cells, channels), F32), shape((32, 2, 16, 128), BF)),
        7,
        smem=(0,),
        flops=blocks * conv_flops,
        name="residual",
    )(flag, arriving, last_value, points, slopes, turned, gain)
    spread = lax.all_to_all(send.reshape(slabs, 16, 128), "layer", 0, 0, tiled=True)
    errors = call(scan_body, shape((slabs, 8, 128), BF), 1, name="scan")(spread)
    error = lax.all_to_all(errors, "layer", 0, 0, tiled=True)
    adjoint, signals = call(
        functools.partial(final_body, width),
        (shape((blocks, cells, channels), F32), shape((images, blocks, 128, 128), BF)),
        8,
        smem=(0,),
        flops=conv_flops,
        name="final",
    )(flag, arriving, last_value, error, gain, relax, slopes, turned)

    received = [lax.dynamic_index_in_dim(signals, here, 0, keepdims=False)]
    for k in range(1, images):
        part = lax.dynamic_index_in_dim(signals, (here + k) % images, 0, keepdims=False)
        received.append(lax.ppermute(part, "dp", [(i, (i + k) % images) for i in range(images)]))
    order = jnp.stack([(here - k) % images for k in range(images)])
    ordered = jnp.take(gathered, order, axis=0)
    states_turned = call(turn_body, shape((blocks, channels, images * cells), BF), 1, name="turn")(ordered)
    grads = call(
        functools.partial(taps_body, width, images),
        shape((blocks, 3, 3, channels, channels // images), F32),
        1 + images,
        flops=blocks * conv_flops,
        name="taps",
    )(states_turned, *received)
    return adjoint.reshape(blocks, 1, height, width, channels), grads


def solution(mesh):
    in_specs = (
        P("layer", "dp", None, None, None),
        P("layer", None, None, None, None),
        P("layer", "dp", None, None, None),
        P("layer", None, None, None),
        P("dp", None, None, None),
    )
    out_specs = (P("layer", "dp", None, None, None), P("layer", None, None, None, "dp"))
    return jax.shard_map(
        on_device, mesh=mesh, in_specs=in_specs, out_specs=out_specs, check_vma=False
    )
```

```python
import functools

import jax
import jax.numpy as jnp
from jax import lax
from jax.experimental import pallas as pl
from jax.experimental.pallas import tpu as pltpu
from jax.sharding import PartitionSpec as P

STEP = 0.5
DAMPING = 0.5
BF = jnp.bfloat16
F32 = jnp.float32
VMEM_LIMIT = 24 * 1024 * 1024


def call(body, outs, n_in, smem=(), flops=0, name=None):
    return pl.pallas_call(
        body,
        out_shape=outs,
        in_specs=[
            pl.BlockSpec(memory_space=pltpu.SMEM if k in smem else pltpu.VMEM)
            for k in range(n_in)
        ],
        out_specs=jax.tree.map(lambda _: pl.BlockSpec(memory_space=pltpu.VMEM), outs),
        compiler_params=pltpu.CompilerParams(vmem_limit_bytes=VMEM_LIMIT),
        cost_estimate=pl.CostEstimate(flops=flops, bytes_accessed=2_000_000, transcendentals=0),
        name=name,
    )


def columns(value, width):
    cells = value.shape[0]
    col = lax.broadcasted_iota(jnp.int32, value.shape, 0) % width
    ahead = jnp.where(col == width - 1, 0.0, pltpu.roll(value, cells - 1, 0))
    behind = jnp.where(col == 0, 0.0, pltpu.roll(value, 1, 0))
    return ahead, value, behind


def rows(value, width):
    edge = jnp.zeros((width, value.shape[1]), value.dtype)
    return jnp.concatenate([edge, value, edge], 0)


def forward_patches(value, width):
    cells = value.shape[0]
    ahead, here, behind = columns(value, width)
    padded = [rows(part.astype(BF), width) for part in (behind, here, ahead)]
    return [padded[j][i * width : i * width + cells] for i in range(3) for j in range(3)]


def adjoint_patches(value, width):
    cells = value.shape[0]
    ahead, here, behind = columns(value, width)
    padded = [rows(part.astype(BF), width) for part in (ahead, here, behind)]
    return [padded[j][(2 - i) * width : (2 - i) * width + cells] for i in range(3) for j in range(3)]


def adjoint_conv(signal, turned_ref, block, width):
    patches = jnp.concatenate(adjoint_patches(signal, width), 1)
    return jnp.dot(patches, turned_ref[block], preferred_element_type=F32)


def block_map(value, slope, turned_ref, block, width):
    signal = (slope * value).astype(BF).astype(F32)
    return value + STEP * adjoint_conv(signal, turned_ref, block, width)


def relaxed(right, slope_ref, turned_ref, width):
    for block in range(slope_ref.shape[0] - 1, -1, -1):
        right = block_map(right, slope_ref[block], turned_ref, block, width)
    return right


def slope_body(width, states_ref, kernels_ref, slope_ref, turned_ref):
    blocks, _, height, _, channels = states_ref.shape
    for block in range(blocks):
        value = states_ref[block, 0].reshape(height * width, channels).astype(F32)
        patches = jnp.concatenate(forward_patches(value, width), 1)
        taps = kernels_ref[block].reshape(9 * channels, channels)
        act = jnp.tanh(jnp.dot(patches, taps, preferred_element_type=F32))
        slope_ref[block] = 1.0 - act * act
        for i in range(3):
            for j in range(3):
                at = (i * 3 + j) * channels
                turned_ref[block, at : at + channels, :] = kernels_ref[block, i, j].T


def entering(flag_ref, arriving_ref, terminal_ref):
    return jnp.where(flag_ref[0] == 1, terminal_ref[...], arriving_ref[...].astype(F32))


def sweep_body(width, flag_ref, arriving_ref, terminal_ref, points_ref, slope_ref, turned_ref, out_ref, send_ref):
    right = entering(flag_ref, arriving_ref, terminal_ref)
    points = points_ref[...]
    points = points + DAMPING * (relaxed(right, slope_ref, turned_ref, width) - points)
    out_ref[...] = points
    send_ref[...] = points.astype(BF)


def residual_body(width, flag_ref, arriving_ref, terminal_ref, points_ref, slope_ref, turned_ref, gain_ref, relax_ref, send_ref):
    right = entering(flag_ref, arriving_ref, terminal_ref)
    relax = relaxed(right, slope_ref, turned_ref, width)
    relax_ref[...] = relax
    residual = (relax - points_ref[...]).reshape(32, 8, 256)
    decay = (1.0 - gain_ref[...]).reshape(32, 8, 256)
    for half in range(2):
        lanes = slice(128 * half, 128 * half + 128)
        send_ref[:, half] = jnp.concatenate([residual[:, :, lanes], decay[:, :, lanes]], 1).astype(BF)


def scan_body(given_ref, out_ref):
    count = given_ref.shape[0]
    error = jnp.zeros((8, 128), F32)
    for at in range(count - 1, -1, -1):
        out_ref[at] = error.astype(BF)
        term = given_ref[at].astype(F32)
        error = error - term[8:] * error + term[:8]


def final_body(width, flag_ref, arriving_ref, terminal_ref, error_ref, gain_ref, relax_ref, slope_ref, turned_ref, adjoint_ref, signal_ref):
    error = error_ref[...].astype(F32).reshape(32, 2, 8, 128)
    error = jnp.concatenate([error[:, 0], error[:, 1]], 2).reshape(256, 256)
    right = entering(flag_ref, arriving_ref, terminal_ref) + error
    adjoint_ref[0] = gain_ref[...] * error + relax_ref[...]
    slope = slope_ref[1]
    last = (slope * right).astype(BF).astype(F32)
    inner = right + STEP * adjoint_conv(last, turned_ref, 1, width)
    adjoint_ref[1] = inner
    first = (slope_ref[0] * inner).astype(BF).astype(F32)
    low = lax.broadcasted_iota(jnp.int32, (128, 128), 1) < 64
    for block, signal in ((0, first), (1, last)):
        for half in range(2):
            top = signal[:128, 128 * half : 128 * half + 128]
            bottom = signal[128:, 128 * half : 128 * half + 128]
            signal_ref[2 * half, block] = jnp.where(low, top, pltpu.roll(bottom, 64, 1)).astype(BF)
            signal_ref[2 * half + 1, block] = jnp.where(low, pltpu.roll(top, 64, 1), bottom).astype(BF)


def turn_body(*refs):
    out_ref = refs[-1]
    for image, states_ref in enumerate(refs[:-1]):
        for block in range(states_ref.shape[0]):
            out_ref[block, :, 256 * image : 256 * image + 256] = states_ref[block].T


def taps_body(width, images, *refs):
    states_ref, signal_refs, out_ref = refs[0], refs[1 : 1 + images], refs[1 + images]
    low = lax.broadcasted_iota(jnp.int32, (128, 128), 1) < 64
    wide = lax.broadcasted_iota(jnp.int32, (256, 128), 1) < 64
    for block in range(out_ref.shape[0]):
        parts = []
        for image in range(images):
            packed = signal_refs[image][block].astype(F32)
            other = pltpu.roll(packed, 64, 1)
            both = jnp.concatenate([jnp.where(low, packed, other), jnp.where(low, other, packed)], 0)
            patches = adjoint_patches(both, width)
            patches.append(patches[-1])
            parts.append(
                jnp.concatenate([jnp.where(wide, patches[2 * k], patches[2 * k + 1]) for k in range(5)], 1)
            )
        moved = jnp.concatenate(parts, 0)
        grads = (STEP * jnp.dot(states_ref[block], moved, preferred_element_type=F32)).T
        for tap in range(9):
            out_ref[block, tap // 3, tap % 3] = grads[64 * tap : 64 * tap + 64]


def on_device(states, kernels, adjoint_guess, coarse_gain, terminal):
    blocks, _, height, width, channels = states.shape
    cells = height * width
    slabs = lax.axis_size("layer")
    images = lax.axis_size("dp")
    here = lax.axis_index("dp")
    flag = (lax.axis_index("layer") == slabs - 1).astype(jnp.int32).reshape(1)
    conv_flops = 2 * cells * 9 * channels * channels
    shape = jax.ShapeDtypeStruct

    def from_right(points):
        return lax.ppermute(points, "layer", [((i + 1) % slabs, i) for i in range(slabs)])

    points = adjoint_guess.reshape(cells, channels)
    last_value = terminal.reshape(cells, channels)
    gain = coarse_gain.reshape(cells, channels)
    arriving = from_right(points)
    slopes, turned = call(
        functools.partial(slope_body, width),
        (shape((blocks, cells, channels), F32), shape((blocks, 9 * channels, channels), BF)),
        2,
        flops=blocks * conv_flops,
        name="slopes",
    )(states, kernels)
    for sweep_index in range(2):
        points, send = call(
            functools.partial(sweep_body, width),
            (shape((cells, channels), F32), shape((cells, channels), BF)),
            6,
            smem=(0,),
            flops=blocks * conv_flops,
            name="sweep",
        )(flag, arriving, last_value, points, slopes, turned)
        arriving = from_right(send)
    relax, send = call(
        functools.partial(residual_body, width),
        (shape((cells, channels), F32), shape((32, 2, 16, 128), BF)),
        7,
        smem=(0,),
        flops=blocks * conv_flops,
        name="residual",
    )(flag, arriving, last_value, points, slopes, turned, gain)
    own_states, send = lax.optimization_barrier((states.reshape(blocks, cells, channels), send))
    spread = lax.all_to_all(send.reshape(slabs, 16, 128), "layer", 0, 0, tiled=True)
    errors = call(scan_body, shape((slabs, 8, 128), BF), 1, name="scan")(spread)
    error = lax.all_to_all(errors, "layer", 0, 0, tiled=True)
    adjoint, signals = call(
        functools.partial(final_body, width),
        (shape((blocks, cells, channels), F32), shape((images, blocks, 128, 128), BF)),
        8,
        smem=(0,),
        flops=conv_flops,
        name="final",
    )(flag, arriving, last_value, error, gain, relax, slopes, turned)

    all_states, received = [own_states], [lax.dynamic_index_in_dim(signals, here, 0, keepdims=False)]
    for k in range(1, images):
        route = [(i, (i + k) % images) for i in range(images)]
        all_states.append(lax.ppermute(own_states, "dp", route))
        part = lax.dynamic_index_in_dim(signals, (here + k) % images, 0, keepdims=False)
        received.append(lax.ppermute(part, "dp", route))
    states_turned = call(
        turn_body, shape((blocks, channels, images * cells), BF), images, name="turn"
    )(*all_states)
    grads = call(
        functools.partial(taps_body, width, images),
        shape((blocks, 3, 3, channels // images, channels), F32),
        1 + images,
        flops=blocks * conv_flops,
        name="taps",
    )(states_turned, *received)
    return adjoint.reshape(blocks, 1, height, width, channels), jnp.swapaxes(grads, 3, 4)


def solution(mesh):
    in_specs = (
        P("layer", "dp", None, None, None),
        P("layer", None, None, None, None),
        P("layer", "dp", None, None, None),
        P("layer", None, None, None),
        P("dp", None, None, None),
    )
    out_specs = (P("layer", "dp", None, None, None), P("layer", None, None, None, "dp"))
    return jax.shard_map(
        on_device, mesh=mesh, in_specs=in_specs, out_specs=out_specs, check_vma=False
    )
```

```python
import functools

import jax
import jax.numpy as jnp
from jax import lax
from jax.experimental import pallas as pl
from jax.experimental.pallas import tpu as pltpu
from jax.sharding import PartitionSpec as P

STEP = 0.5
DAMPING = 0.5
BF = jnp.bfloat16
F32 = jnp.float32
VMEM_LIMIT = 12 * 1024 * 1024


def call(body, outs, ins, flops=0, moved=2_000_000, name=None, scratch=(), far_in=(), far_out=(), alias=None):
    def spec(far):
        return pl.BlockSpec(memory_space=pltpu.HBM if far else pltpu.VMEM)

    single = not isinstance(outs, tuple)
    placed = tuple(
        (pltpu.HBM if k in far_out else pltpu.VMEM)(out.shape, out.dtype)
        for k, out in enumerate((outs,) if single else outs)
    )
    ins = [
        pltpu.with_memory_space_constraint(value, pltpu.HBM if k in far_in else pltpu.VMEM)
        for k, value in enumerate(ins)
    ]
    out_specs = [spec(k in far_out) for k in range(1 if single else len(outs))]
    return pl.pallas_call(
        body,
        out_shape=placed[0] if single else placed,
        in_specs=[spec(k in far_in) for k in range(len(ins))],
        out_specs=out_specs[0] if single else tuple(out_specs),
        scratch_shapes=scratch,
        input_output_aliases=alias or {},
        compiler_params=pltpu.CompilerParams(vmem_limit_bytes=VMEM_LIMIT),
        cost_estimate=pl.CostEstimate(flops=flops, bytes_accessed=moved, transcendentals=0),
        name=name,
    )(*ins)


def is_even():
    return lax.axis_index("layer") % 2 == 0


def is_last():
    return lax.axis_index("layer") == lax.axis_size("layer") - 1


def columns(value, width):
    cells = value.shape[0]
    col = lax.broadcasted_iota(jnp.int32, value.shape, 0) % width
    ahead = jnp.where(col == width - 1, 0.0, pltpu.roll(value, cells - 1, 0))
    behind = jnp.where(col == 0, 0.0, pltpu.roll(value, 1, 0))
    return ahead, value, behind


def rows(value, width):
    edge = jnp.zeros((width, value.shape[1]), value.dtype)
    return jnp.concatenate([edge, value, edge], 0)


def forward_patches(value, width):
    cells = value.shape[0]
    ahead, here, behind = columns(value, width)
    padded = [rows(part.astype(BF), width) for part in (behind, here, ahead)]
    return [padded[j][i * width : i * width + cells] for i in range(3) for j in range(3)]


def adjoint_patches(value, width):
    cells = value.shape[0]
    ahead, here, behind = columns(value, width)
    padded = [rows(part.astype(BF), width) for part in (ahead, here, behind)]
    return [padded[j][(2 - i) * width : (2 - i) * width + cells] for i in range(3) for j in range(3)]


def adjoint_conv(signal, turned_ref, block, width):
    patches = jnp.concatenate(adjoint_patches(signal, width), 1)
    return jnp.dot(patches, turned_ref[block], preferred_element_type=F32)


def block_map(value, slope, turned_ref, block, width):
    signal = (slope * value).astype(BF).astype(F32)
    return value + STEP * adjoint_conv(signal, turned_ref, block, width)


def relaxed(right, slope_ref, turned_ref, width):
    for block in range(turned_ref.shape[0] - 1, -1, -1):
        right = block_map(right, slope_ref[block], turned_ref, block, width)
    return right


def slope_body(width, states_far, kernels_far, points_far, slope_ref, turned_ref, points_ref, states_ref, kernels_ref, sems):
    blocks, height, _, channels = states_ref.shape
    held = [pltpu.make_async_copy(states_far.at[:, 0], states_ref, sems.at[blocks])]
    for block in range(blocks):
        held.append(pltpu.make_async_copy(kernels_far.at[block], kernels_ref.at[block], sems.at[block]))
    held.append(pltpu.make_async_copy(points_far, points_ref, sems.at[blocks + 1]))
    for copy in held:
        copy.start()
    held[0].wait()
    for block in range(blocks):
        value = states_ref[block].reshape(height * width, channels).astype(F32)
        patches = jnp.concatenate(forward_patches(value, width), 1)
        held[1 + block].wait()
        taps = kernels_ref[block].reshape(9 * channels, channels)
        act = jnp.tanh(jnp.dot(patches, taps, preferred_element_type=F32))
        slope_ref[block] = 1.0 - act * act
        for i in range(3):
            for j in range(3):
                at = (i * 3 + j) * channels
                turned_ref[block, at : at + channels, :] = kernels_ref[block, i, j].T
    held[-1].wait()


def fetch(far_ref, near_ref, sem):
    copy = pltpu.make_async_copy(far_ref, near_ref, sem)
    copy.start()
    copy.wait()


def enter(right_ref, swapped_ref, crossed_ref, terminal_far, sem):
    @pl.when(is_even())
    def _():
        right_ref[...] = swapped_ref[...].astype(F32)

    @pl.when(jnp.logical_not(jnp.logical_or(is_even(), is_last())))
    def _():
        right_ref[...] = crossed_ref[...].astype(F32)

    @pl.when(is_last())
    def _():
        fetch(terminal_far, right_ref, sem)


def sweep(right, slope_ref, turned_ref, points_ref, width):
    points = points_ref[...]
    points_ref[...] = points + DAMPING * (relaxed(right, slope_ref, turned_ref, width) - points)


def even_body(width, swapped_ref, slope_ref, turned_ref, _, points_ref, send_ref):
    @pl.when(is_even())
    def _():
        sweep(swapped_ref[...].astype(F32), slope_ref, turned_ref, points_ref, width)

    send_ref[...] = points_ref[...].astype(BF)


def odd_body(width, crossed_ref, terminal_far, slope_ref, turned_ref, _, points_ref, send_ref, right_ref, sem):
    @pl.when(is_last())
    def _():
        fetch(terminal_far, right_ref, sem)

    @pl.when(jnp.logical_not(jnp.logical_or(is_even(), is_last())))
    def _():
        right_ref[...] = crossed_ref[...].astype(F32)

    @pl.when(jnp.logical_not(is_even()))
    def _():
        sweep(right_ref[...], slope_ref, turned_ref, points_ref, width)

    send_ref[...] = points_ref[...].astype(BF)


def sweep_body(width, swapped_ref, crossed_ref, terminal_far, slope_ref, turned_ref, _, points_ref, send_ref, right_ref, sem):
    enter(right_ref, swapped_ref, crossed_ref, terminal_far, sem)
    sweep(right_ref[...], slope_ref, turned_ref, points_ref, width)
    send_ref[...] = points_ref[...].astype(BF)


def residual_body(width, swapped_ref, crossed_ref, terminal_far, slope_ref, turned_ref, _, gain_far, relax_far, send_far, points_ref, right_ref, gain_ref, relax_ref, send_ref, sem, sems):
    gain_copy = pltpu.make_async_copy(gain_far, gain_ref, sems.at[0])
    gain_copy.start()
    enter(right_ref, swapped_ref, crossed_ref, terminal_far, sem)
    right = right_ref[...]
    relax = relaxed(right, slope_ref, turned_ref, width)
    residual = (relax - points_ref[...]).reshape(32, 8, 256)
    gain_copy.wait()
    decay = (1.0 - gain_ref[...]).reshape(32, 8, 256)
    for half in range(2):
        lanes = slice(128 * half, 128 * half + 128)
        send_ref[:, half] = jnp.concatenate([residual[:, :, lanes], decay[:, :, lanes]], 1).astype(BF)
    send_copy = pltpu.make_async_copy(send_ref, send_far, sems.at[1])
    send_copy.start()
    relax_ref[...] = relax
    relax_copy = pltpu.make_async_copy(relax_ref, relax_far, sems.at[2])
    relax_copy.start()
    points_ref[...] = right
    send_copy.wait()
    relax_copy.wait()


def scan_body(given_ref, out_far, out_ref, sem):
    count = given_ref.shape[0]
    error = jnp.zeros((8, 128), F32)
    for at in range(count - 1, -1, -1):
        out_ref[at] = error.astype(BF)
        term = given_ref[at].astype(F32)
        error = error - term[8:] * error + term[:8]
    copy = pltpu.make_async_copy(out_ref, out_far, sem)
    copy.start()
    copy.wait()


def final_body(width, points_ref, error_ref, slope_ref, turned_ref, inner_ref, error_out_ref, signal_ref):
    error = error_ref[...].astype(F32).reshape(32, 2, 8, 128)
    error = jnp.concatenate([error[:, 0], error[:, 1]], 2).reshape(256, 256)
    error_out_ref[...] = error
    right = points_ref[...] + error
    last = (slope_ref[1] * right).astype(BF).astype(F32)
    inner = right + STEP * adjoint_conv(last, turned_ref, 1, width)
    inner_ref[...] = inner
    first = (slope_ref[0] * inner).astype(BF).astype(F32)
    low = lax.broadcasted_iota(jnp.int32, (128, 128), 1) < 64
    for block, signal in ((0, first), (1, last)):
        for half in range(2):
            top = signal[:128, 128 * half : 128 * half + 128]
            bottom = signal[128:, 128 * half : 128 * half + 128]
            signal_ref[2 * half, block] = jnp.where(low, top, pltpu.roll(bottom, 64, 1)).astype(BF)
            signal_ref[2 * half + 1, block] = jnp.where(low, pltpu.roll(top, 64, 1), bottom).astype(BF)


def corrected_body(error_ref, gain_ref, relax_ref, inner_ref, adjoint_far, out_ref, sems):
    inner_copy = pltpu.make_async_copy(inner_ref, adjoint_far.at[1], sems.at[1])
    inner_copy.start()
    out_ref[...] = gain_ref[...] * error_ref[...] + relax_ref[...]
    out_copy = pltpu.make_async_copy(out_ref, adjoint_far.at[0], sems.at[0])
    out_copy.start()
    inner_copy.wait()
    out_copy.wait()


def turn_body(*refs):
    out_ref = refs[-1]
    for image, states_ref in enumerate(refs[:-1]):
        for block in range(states_ref.shape[0]):
            out_ref[block, :, 256 * image : 256 * image + 256] = states_ref[block].T


def taps_body(width, *refs, images):
    states_ref, signal_refs = refs[0], refs[1 : 1 + images]
    out_far, out_ref, sems = refs[1 + images :]
    copies = []
    low = lax.broadcasted_iota(jnp.int32, (128, 128), 1) < 64
    wide = lax.broadcasted_iota(jnp.int32, (256, 128), 1) < 64
    for block in range(out_ref.shape[0]):
        parts = []
        for image in range(images):
            packed = signal_refs[image][block].astype(F32)
            other = pltpu.roll(packed, 64, 1)
            both = jnp.concatenate([jnp.where(low, packed, other), jnp.where(low, other, packed)], 0)
            patches = adjoint_patches(both, width)
            patches.append(patches[-1])
            parts.append(
                jnp.concatenate([jnp.where(wide, patches[2 * k], patches[2 * k + 1]) for k in range(5)], 1)
            )
        moved = jnp.concatenate(parts, 0)
        grads = (STEP * jnp.dot(states_ref[block], moved, preferred_element_type=F32)).T
        for tap in range(9):
            out_ref[block, tap // 3, tap % 3] = grads[64 * tap : 64 * tap + 64]
        copies.append(pltpu.make_async_copy(out_ref.at[block], out_far.at[block], sems.at[block]))
        copies[-1].start()
    for copy in copies:
        copy.wait()


def on_device(states, kernels, adjoint_guess, coarse_gain, terminal):
    blocks, _, height, width, channels = states.shape
    cells = height * width
    slabs = lax.axis_size("layer")
    images = lax.axis_size("dp")
    here = lax.axis_index("dp")
    slab = lax.axis_index("layer")
    conv_flops = 2 * cells * 9 * channels * channels
    shape = jax.ShapeDtypeStruct

    def swapped(part):
        return lax.ppermute(part, "layer", [(i ^ 1, i) for i in range(slabs)])

    def crossed(part):
        route = [((i + 1) % slabs if i % 2 else (i - 1) % slabs, i) for i in range(slabs)]
        return lax.ppermute(part, "layer", route)

    whole = shape((cells, channels), F32)
    rounded = shape((cells, channels), BF)

    def step(body, outs, *ins, name, **more):
        return call(functools.partial(body, width), outs, ins, flops=blocks * conv_flops, name=name, **more)

    def right_of(part):
        return jnp.where(slab == slabs - 1, jnp.zeros_like(part), part)

    points = adjoint_guess.reshape(cells, channels)
    last_value = terminal.reshape(cells, channels)
    gain = coarse_gain.reshape(cells, channels)
    rough = points.astype(BF)
    across, beside = crossed(rough), swapped(rough)
    slopes, turned, points = step(
        slope_body,
        (shape((blocks, cells, channels), F32), shape((blocks, 9 * channels, channels), BF), whole),
        states,
        kernels,
        points,
        name="slopes",
        far_in=(0, 1, 2),
        scratch=(
            pltpu.VMEM((blocks, height, width, channels), BF),
            pltpu.VMEM((blocks, 3, 3, channels, channels), BF),
            pltpu.SemaphoreType.DMA((blocks + 2,)),
        ),
    )
    points, send = step(
        even_body, (whole, rounded), beside, slopes, turned, points, name="even", alias={3: 0}
    )
    next_across = crossed(send)
    right_scratch = (pltpu.VMEM((cells, channels), F32), pltpu.SemaphoreType.DMA)
    points, send = step(
        odd_body,
        (whole, rounded),
        across,
        last_value,
        slopes,
        turned,
        points,
        name="odd",
        alias={4: 0},
        far_in=(1,),
        scratch=right_scratch,
    )
    beside, across = swapped(send), right_of(next_across)
    points, send = step(
        sweep_body,
        (whole, rounded),
        beside,
        across,
        last_value,
        slopes,
        turned,
        points,
        name="sweep",
        alias={5: 0},
        far_in=(2,),
        scratch=right_scratch,
    )
    across, beside = right_of(crossed(send)), swapped(send)
    packed = (32, 2, 16, 128)
    relax, send, points = step(
        residual_body,
        (whole, shape(packed, BF), whole),
        beside,
        across,
        last_value,
        slopes,
        turned,
        points,
        gain,
        name="residual",
        far_in=(2, 6),
        far_out=(0, 1),
        alias={5: 2},
        scratch=(
            pltpu.VMEM((cells, channels), F32),
            pltpu.VMEM((cells, channels), F32),
            pltpu.VMEM((cells, channels), F32),
            pltpu.VMEM(packed, BF),
            pltpu.SemaphoreType.DMA,
            pltpu.SemaphoreType.DMA((3,)),
        ),
    )

    def spread(parts):
        return lax.all_to_all(parts, "layer", 0, 0, tiled=True)

    own_states, send = lax.optimization_barrier((states.reshape(blocks, cells, channels), send))
    errors = call(
        scan_body,
        shape((slabs, 8, 128), BF),
        (spread(send.reshape(slabs, 16, 128)),),
        name="scan",
        moved=0,
        far_out=(0,),
        scratch=(pltpu.VMEM((slabs, 8, 128), BF), pltpu.SemaphoreType.DMA),
    )
    error = spread(errors)
    all_states = [own_states]
    for k in range(1, images):
        all_states.append(lax.ppermute(own_states, "dp", [(i, (i + k) % images) for i in range(images)]))
    states_turned = call(
        turn_body, shape((blocks, channels, images * cells), BF), all_states, name="turn"
    )
    error, states_turned = lax.optimization_barrier((error, states_turned))
    inner, error, signals = step(
        final_body,
        (whole, whole, shape((images, blocks, 128, 128), BF)),
        points,
        error,
        slopes,
        turned,
        name="final",
    )

    received = [lax.dynamic_index_in_dim(signals, here, 0, keepdims=False)]
    for k in range(1, images):
        part = lax.dynamic_index_in_dim(signals, (here + k) % images, 0, keepdims=False)
        received.append(lax.ppermute(part, "dp", [(i, (i + k) % images) for i in range(images)]))
    adjoint = call(
        corrected_body, shape((blocks, cells, channels), F32), (error, gain, relax, inner), name="corrected", far_out=(0,),
        scratch=(pltpu.VMEM((cells, channels), F32), pltpu.SemaphoreType.DMA((2,))),
    )
    slices = (blocks, 3, 3, channels // images, channels)
    grads = step(
        functools.partial(taps_body, images=images),
        shape(slices, F32),
        states_turned,
        *received,
        name="taps",
        far_out=(0,),
        scratch=(pltpu.VMEM(slices, F32), pltpu.SemaphoreType.DMA((blocks,))),
    )
    return adjoint.reshape(blocks, 1, height, width, channels), jnp.swapaxes(grads, 3, 4)


def solution(mesh):
    in_specs = (
        P("layer", "dp", None, None, None),
        P("layer", None, None, None, None),
        P("layer", "dp", None, None, None),
        P("layer", None, None, None),
        P("dp", None, None, None),
    )
    out_specs = (P("layer", "dp", None, None, None), P("layer", None, None, None, "dp"))
    return jax.shard_map(
        on_device, mesh=mesh, in_specs=in_specs, out_specs=out_specs, check_vma=False
    )
```

```python
import functools

import jax
import jax.numpy as jnp
from jax import lax
from jax.experimental import pallas as pl
from jax.experimental.pallas import tpu as pltpu
from jax.sharding import PartitionSpec as P

STEP = 0.5
DAMPING = 0.5
BF = jnp.bfloat16
F32 = jnp.float32
VMEM_LIMIT = 12 * 1024 * 1024


def call(body, outs, ins, flops=0, moved=2_000_000, name=None, scratch=(), far_in=(), far_out=(), alias=None):
    def spec(far):
        return pl.BlockSpec(memory_space=pltpu.HBM if far else pltpu.VMEM)

    single = not isinstance(outs, tuple)
    placed = tuple(
        (pltpu.HBM if k in far_out else pltpu.VMEM)(out.shape, out.dtype)
        for k, out in enumerate((outs,) if single else outs)
    )
    ins = [
        pltpu.with_memory_space_constraint(value, pltpu.HBM if k in far_in else pltpu.VMEM)
        for k, value in enumerate(ins)
    ]
    out_specs = [spec(k in far_out) for k in range(1 if single else len(outs))]
    return pl.pallas_call(
        body,
        out_shape=placed[0] if single else placed,
        in_specs=[spec(k in far_in) for k in range(len(ins))],
        out_specs=out_specs[0] if single else tuple(out_specs),
        scratch_shapes=scratch,
        input_output_aliases=alias or {},
        compiler_params=pltpu.CompilerParams(vmem_limit_bytes=VMEM_LIMIT),
        cost_estimate=pl.CostEstimate(flops=flops, bytes_accessed=moved, transcendentals=0),
        name=name,
    )(*ins)


def is_even():
    return lax.axis_index("layer") % 2 == 0


def stage(body):
    pl.when(lax.axis_index("layer") >= 0)(body)


def is_first():
    return lax.axis_index("layer") == 0


def columns(value, width):
    cells = value.shape[0]
    col = lax.broadcasted_iota(jnp.int32, value.shape, 0) % width
    ahead = jnp.where(col == width - 1, 0.0, pltpu.roll(value, cells - 1, 0))
    behind = jnp.where(col == 0, 0.0, pltpu.roll(value, 1, 0))
    return ahead, value, behind


def rows(value, width):
    edge = jnp.zeros((width, value.shape[1]), value.dtype)
    return jnp.concatenate([edge, value, edge], 0)


def forward_patches(value, width):
    cells = value.shape[0]
    ahead, here, behind = columns(value, width)
    padded = [rows(part.astype(BF), width) for part in (behind, here, ahead)]
    return [padded[j][i * width : i * width + cells] for i in range(3) for j in range(3)]


def adjoint_patches(value, width):
    cells = value.shape[0]
    ahead, here, behind = columns(value, width)
    padded = [rows(part.astype(BF), width) for part in (ahead, here, behind)]
    return [padded[j][(2 - i) * width : (2 - i) * width + cells] for i in range(3) for j in range(3)]


def adjoint_conv(signal, turned_ref, block, width):
    patches = jnp.concatenate(adjoint_patches(signal, width), 1)
    return jnp.dot(patches, turned_ref[block], preferred_element_type=F32)


def block_map(value, slope, turned_ref, block, width):
    signal = (slope * value).astype(BF).astype(F32)
    return value + STEP * adjoint_conv(signal, turned_ref, block, width)


def relaxed(right, slope_ref, turned_ref, width):
    for block in range(turned_ref.shape[0] - 1, -1, -1):
        right = block_map(right, slope_ref[block], turned_ref, block, width)
    return right


def round_body(width, points_far, terminal_far, out_ref, held_ref, sem):
    edge = pltpu.make_async_copy(terminal_far, held_ref, sem)
    plain = pltpu.make_async_copy(points_far, held_ref, sem)
    pl.when(is_first())(edge.start)
    pl.when(jnp.logical_not(is_first()))(plain.start)
    plain.wait()
    out_ref[...] = held_ref[...].astype(BF)


def slope_body(width, states_far, kernels_far, points_far, slope_ref, turned_ref, points_ref, states_ref, kernels_ref, sems):
    blocks, height, _, channels = states_ref.shape
    held = [pltpu.make_async_copy(states_far.at[:, 0], states_ref, sems.at[3 * blocks])]
    for block in range(blocks):
        for i in range(3):
            sem = sems.at[3 * block + i]
            held.append(pltpu.make_async_copy(kernels_far.at[block, i], kernels_ref.at[block, i], sem))
    held.append(pltpu.make_async_copy(points_far, points_ref, sems.at[3 * blocks + 1]))
    for copy in held:
        copy.start()
    held[0].wait()


    def one(block):
        for i in range(3):
            held[1 + 3 * block + i].wait()
        value = states_ref[block].reshape(height * width, channels).astype(F32)
        patches = jnp.concatenate(forward_patches(value, width), 1)
        taps = kernels_ref[block].reshape(9 * channels, channels)
        act = jnp.tanh(jnp.dot(patches, taps, preferred_element_type=F32))
        slope_ref[block] = (1.0 - act * act).astype(BF)
        for i in range(3):
            for j in range(3):
                at = (i * 3 + j) * channels
                turned_ref[block, at : at + channels, :] = kernels_ref[block, i, j].T

    for block in range(blocks):
        stage(functools.partial(one, block))
    held[-1].wait()


def entering(swapped_ref, shifted_ref):
    return jnp.where(is_even(), swapped_ref[...], shifted_ref[...]).astype(F32)


class Edge:
    def __init__(self, terminal_far, edge_ref, sem):
        self.copy = pltpu.make_async_copy(terminal_far, edge_ref, sem)
        self.edge_ref = edge_ref
        pl.when(is_first())(self.copy.start)

    def write(self, points_ref, send_ref):
        @pl.when(is_first())
        def _():
            self.copy.wait()
            send_ref[...] = self.edge_ref[...].astype(BF)

        @pl.when(jnp.logical_not(is_first()))
        def _():
            send_ref[...] = points_ref[...].astype(BF)


def sweep(right, slope_ref, turned_ref, points_ref, width):
    points = points_ref[...]
    points_ref[...] = points + DAMPING * (relaxed(right, slope_ref, turned_ref, width) - points)


def even_body(width, swapped_ref, terminal_far, slope_ref, turned_ref, _, points_ref, send_ref, edge_ref, sem):
    edge = Edge(terminal_far, edge_ref, sem)

    @pl.when(is_even())
    def _():
        sweep(swapped_ref[...].astype(F32), slope_ref, turned_ref, points_ref, width)

    edge.write(points_ref, send_ref)


def odd_body(width, shifted_ref, slope_ref, turned_ref, _, points_ref, send_ref):
    @pl.when(jnp.logical_not(is_even()))
    def _():
        sweep(shifted_ref[...].astype(F32), slope_ref, turned_ref, points_ref, width)

    send_ref[...] = points_ref[...].astype(BF)


def sweep_body(width, swapped_ref, shifted_ref, terminal_far, slope_ref, turned_ref, _, points_ref, send_ref, edge_ref, sem):
    edge = Edge(terminal_far, edge_ref, sem)
    sweep(entering(swapped_ref, shifted_ref), slope_ref, turned_ref, points_ref, width)
    edge.write(points_ref, send_ref)


def residual_body(width, shifted_ref, slope_ref, turned_ref, _, gain_far, relax_far, send_far, points_ref, gain_ref, relax_ref, send_ref, sems):
    gain_copy = pltpu.make_async_copy(gain_far, gain_ref, sems.at[0])
    gain_copy.start()
    relax_copy = pltpu.make_async_copy(relax_ref, relax_far, sems.at[2])

    @stage
    def _():
        relax_ref[...] = relaxed(shifted_ref[...].astype(F32), slope_ref, turned_ref, width)

    @stage
    def _():
        gain_copy.wait()
        residual = (relax_ref[...] - points_ref[...]).reshape(32, 8, 256)
        decay = (1.0 - gain_ref[...]).reshape(32, 8, 256)
        for half in range(2):
            lanes = slice(128 * half, 128 * half + 128)
            send_ref[:, half] = jnp.concatenate([residual[:, :, lanes], decay[:, :, lanes]], 1).astype(BF)
        send_copy = pltpu.make_async_copy(send_ref, send_far, sems.at[1])
        send_copy.start()
        relax_copy.start()
        points_ref[...] = shifted_ref[...].astype(F32)
        send_copy.wait()
        relax_copy.wait()


def scan_body(given_ref, out_far, out_ref, sem):
    count = given_ref.shape[0]
    error = jnp.zeros((8, 128), F32)
    for at in range(count - 1, -1, -1):
        out_ref[at] = error.astype(BF)
        term = given_ref[at].astype(F32)
        error = error - term[8:] * error + term[:8]
    copy = pltpu.make_async_copy(out_ref, out_far, sem)
    copy.start()
    copy.wait()


def final_body(width, points_ref, error_ref, slope_ref, turned_ref, inner_ref, error_out_ref, signal_ref):
    error = error_ref[...].astype(F32).reshape(32, 2, 8, 128)
    error = jnp.concatenate([error[:, 0], error[:, 1]], 2).reshape(256, 256)
    error_out_ref[...] = error
    right = points_ref[...] + error
    last = (slope_ref[1] * right).astype(BF).astype(F32)
    inner = right + STEP * adjoint_conv(last, turned_ref, 1, width)
    inner_ref[...] = inner
    first = (slope_ref[0] * inner).astype(BF).astype(F32)
    low = lax.broadcasted_iota(jnp.int32, (128, 128), 1) < 64
    for block, signal in ((0, first), (1, last)):
        for half in range(2):
            top = signal[:128, 128 * half : 128 * half + 128]
            bottom = signal[128:, 128 * half : 128 * half + 128]
            signal_ref[2 * half, block] = jnp.where(low, top, pltpu.roll(bottom, 64, 1)).astype(BF)
            signal_ref[2 * half + 1, block] = jnp.where(low, pltpu.roll(top, 64, 1), bottom).astype(BF)


def corrected_body(error_ref, gain_ref, relax_ref, inner_ref, adjoint_far, out_ref, sems):
    inner_copy = pltpu.make_async_copy(inner_ref, adjoint_far.at[1], sems.at[1])
    inner_copy.start()
    out_ref[...] = gain_ref[...] * error_ref[...] + relax_ref[...]
    out_copy = pltpu.make_async_copy(out_ref, adjoint_far.at[0], sems.at[0])
    out_copy.start()
    inner_copy.wait()
    out_copy.wait()


def turn_body(*refs):
    out_ref = refs[-1]
    for image, states_ref in enumerate(refs[:-1]):
        for block in range(states_ref.shape[0]):
            out_ref[block, :, 256 * image : 256 * image + 256] = states_ref[block].T


def taps_body(width, *refs, images):
    states_ref, signal_refs = refs[0], refs[1 : 1 + images]
    out_far, out_ref, sems = refs[1 + images :]
    low = lax.broadcasted_iota(jnp.int32, (128, 128), 1) < 64
    wide = lax.broadcasted_iota(jnp.int32, (256, 128), 1) < 64
    copies = [
        pltpu.make_async_copy(out_ref.at[block], out_far.at[block], sems.at[block])
        for block in range(out_ref.shape[0])
    ]

    def one(block):
        parts = []
        for image in range(images):
            packed = signal_refs[image][block].astype(F32)
            other = pltpu.roll(packed, 64, 1)
            both = jnp.concatenate([jnp.where(low, packed, other), jnp.where(low, other, packed)], 0)
            patches = adjoint_patches(both, width)
            patches.append(patches[-1])
            parts.append(
                jnp.concatenate([jnp.where(wide, patches[2 * k], patches[2 * k + 1]) for k in range(5)], 1)
            )
        moved = jnp.concatenate(parts, 0)
        grads = (STEP * jnp.dot(states_ref[block], moved, preferred_element_type=F32)).T
        for tap in range(9):
            out_ref[block, tap // 3, tap % 3] = grads[64 * tap : 64 * tap + 64]
        copies[block].start()

    for block in range(out_ref.shape[0]):
        stage(functools.partial(one, block))
    for copy in copies:
        copy.wait()


def on_device(states, kernels, adjoint_guess, coarse_gain, terminal):
    blocks, _, height, width, channels = states.shape
    cells = height * width
    slabs = lax.axis_size("layer")
    images = lax.axis_size("dp")
    here = lax.axis_index("dp")
    slab = lax.axis_index("layer")
    conv_flops = 2 * cells * 9 * channels * channels
    shape = jax.ShapeDtypeStruct

    def swapped(part):
        return lax.ppermute(part, "layer", [(i ^ 1, i) for i in range(slabs)])

    def shifted(part):
        return lax.ppermute(part, "layer", [((i + 1) % slabs, i) for i in range(slabs)])

    whole = shape((cells, channels), F32)
    rounded = shape((cells, channels), BF)

    def step(body, outs, *ins, name, **more):
        return call(functools.partial(body, width), outs, ins, flops=blocks * conv_flops, name=name, **more)

    points = adjoint_guess.reshape(cells, channels)
    last_value = terminal.reshape(cells, channels)
    gain = coarse_gain.reshape(cells, channels)
    edge = (pltpu.VMEM((cells, channels), F32), pltpu.SemaphoreType.DMA)
    rough = step(round_body, rounded, points, last_value, name="round", far_in=(0, 1), scratch=edge)
    across, beside = shifted(rough), swapped(rough)
    slopes, turned, points = step(
        slope_body,
        (shape((blocks, cells, channels), BF), shape((blocks, 9 * channels, channels), BF), whole),
        states,
        kernels,
        points,
        name="slopes",
        far_in=(0, 1, 2),
        scratch=(
            pltpu.VMEM((blocks, height, width, channels), BF),
            pltpu.VMEM((blocks, 3, 3, channels, channels), BF),
            pltpu.SemaphoreType.DMA((3 * blocks + 2,)),
        ),
    )
    points, send = step(
        even_body,
        (whole, rounded),
        beside,
        last_value,
        slopes,
        turned,
        points,
        name="even",
        alias={4: 0},
        far_in=(1,),
        scratch=edge,
    )
    next_across = shifted(send)
    points, send = step(
        odd_body, (whole, rounded), across, slopes, turned, points, name="odd", alias={3: 0}
    )
    across = jnp.where(slab == slabs, jnp.zeros_like(next_across), next_across)
    points, send = step(
        sweep_body,
        (whole, rounded),
        swapped(send),
        across,
        last_value,
        slopes,
        turned,
        points,
        name="sweep",
        alias={5: 0},
        far_in=(2,),
        scratch=edge,
    )
    across = shifted(send)
    packed = (32, 2, 16, 128)
    relax, send, points = step(
        residual_body,
        (whole, shape(packed, BF), whole),
        across,
        slopes,
        turned,
        points,
        gain,
        name="residual",
        far_in=(4,),
        far_out=(0, 1),
        alias={3: 2},
        scratch=(
            pltpu.VMEM((cells, channels), F32),
            pltpu.VMEM((cells, channels), F32),
            pltpu.VMEM(packed, BF),
            pltpu.SemaphoreType.DMA((3,)),
        ),
    )

    def spread(parts):
        return lax.all_to_all(parts, "layer", 0, 0, tiled=True)

    own_states, send = lax.optimization_barrier((states.reshape(blocks, cells, channels), send))
    errors = call(
        scan_body,
        shape((slabs, 8, 128), BF),
        (spread(send.reshape(slabs, 16, 128)),),
        name="scan",
        moved=0,
        far_out=(0,),
        scratch=(pltpu.VMEM((slabs, 8, 128), BF), pltpu.SemaphoreType.DMA),
    )
    error = spread(errors)
    all_states = [own_states]
    for k in range(1, images):
        all_states.append(lax.ppermute(own_states, "dp", [(i, (i + k) % images) for i in range(images)]))
    states_turned = call(
        turn_body, shape((blocks, channels, images * cells), BF), all_states, name="turn"
    )
    error, states_turned = lax.optimization_barrier((error, states_turned))
    inner, error, signals = step(
        final_body,
        (whole, whole, shape((images, blocks, 128, 128), BF)),
        points,
        error,
        slopes,
        turned,
        name="final",
    )

    received = [lax.dynamic_index_in_dim(signals, here, 0, keepdims=False)]
    for k in range(1, images):
        part = lax.dynamic_index_in_dim(signals, (here + k) % images, 0, keepdims=False)
        received.append(lax.ppermute(part, "dp", [(i, (i + k) % images) for i in range(images)]))
    adjoint = call(
        corrected_body, shape((blocks, cells, channels), F32), (error, gain, relax, inner), name="corrected", far_out=(0,),
        scratch=(pltpu.VMEM((cells, channels), F32), pltpu.SemaphoreType.DMA((2,))),
    )
    slices = (blocks, 3, 3, channels // images, channels)
    grads = step(
        functools.partial(taps_body, images=images),
        shape(slices, F32),
        states_turned,
        *received,
        name="taps",
        far_out=(0,),
        scratch=(pltpu.VMEM(slices, F32), pltpu.SemaphoreType.DMA((blocks,))),
    )
    return adjoint.reshape(blocks, 1, height, width, channels), jnp.swapaxes(grads, 3, 4)


def solution(mesh):
    in_specs = (
        P("layer", "dp", None, None, None),
        P("layer", None, None, None, None),
        P("layer", "dp", None, None, None),
        P("layer", None, None, None),
        P("dp", None, None, None),
    )
    out_specs = (P("layer", "dp", None, None, None), P("layer", None, None, None, "dp"))
    return jax.shard_map(
        on_device, mesh=mesh, in_specs=in_specs, out_specs=out_specs, check_vma=False
    )
```

```python
import functools

import jax
import jax.numpy as jnp
from jax import lax
from jax.experimental import pallas as pl
from jax.experimental.pallas import tpu as pltpu
from jax.sharding import PartitionSpec as P

STEP = 0.5
DAMPING = 0.5
BF = jnp.bfloat16
F32 = jnp.float32
VMEM_LIMIT = 12 * 1024 * 1024


def call(body, outs, ins, flops=0, moved=2_000_000, name=None, scratch=(), far_in=(), far_out=(), alias=None):
    def spec(far):
        return pl.BlockSpec(memory_space=pltpu.HBM if far else pltpu.VMEM)

    single = not isinstance(outs, tuple)
    placed = tuple(
        (pltpu.HBM if k in far_out else pltpu.VMEM)(out.shape, out.dtype)
        for k, out in enumerate((outs,) if single else outs)
    )
    ins = [
        pltpu.with_memory_space_constraint(value, pltpu.HBM if k in far_in else pltpu.VMEM)
        for k, value in enumerate(ins)
    ]
    out_specs = [spec(k in far_out) for k in range(1 if single else len(outs))]
    return pl.pallas_call(
        body,
        out_shape=placed[0] if single else placed,
        in_specs=[spec(k in far_in) for k in range(len(ins))],
        out_specs=out_specs[0] if single else tuple(out_specs),
        scratch_shapes=scratch,
        input_output_aliases=alias or {},
        compiler_params=pltpu.CompilerParams(vmem_limit_bytes=VMEM_LIMIT),
        cost_estimate=pl.CostEstimate(flops=flops, bytes_accessed=moved, transcendentals=0),
        name=name,
    )(*ins)


def is_even():
    return lax.axis_index("layer") % 2 == 0


def stage(body):
    pl.when(lax.axis_index("layer") >= 0)(body)


def is_first():
    return lax.axis_index("layer") == 0


def columns(value, width):
    cells = value.shape[0]
    col = lax.broadcasted_iota(jnp.int32, value.shape, 0) % width
    ahead = jnp.where(col == width - 1, 0.0, pltpu.roll(value, cells - 1, 0))
    behind = jnp.where(col == 0, 0.0, pltpu.roll(value, 1, 0))
    return ahead, value, behind


def rows(value, width):
    edge = jnp.zeros((width, value.shape[1]), value.dtype)
    return jnp.concatenate([edge, value, edge], 0)


def forward_patches(value, width):
    cells = value.shape[0]
    ahead, here, behind = columns(value, width)
    padded = [rows(part.astype(BF), width) for part in (behind, here, ahead)]
    return [padded[j][i * width : i * width + cells] for i in range(3) for j in range(3)]


def adjoint_patches(value, width):
    cells = value.shape[0]
    ahead, here, behind = columns(value, width)
    padded = [rows(part.astype(BF), width) for part in (ahead, here, behind)]
    return [padded[j][(2 - i) * width : (2 - i) * width + cells] for i in range(3) for j in range(3)]


def adjoint_conv(signal, turned_ref, block, width):
    patches = jnp.concatenate(adjoint_patches(signal, width), 1)
    return jnp.dot(patches, turned_ref[block], preferred_element_type=F32)


def block_map(value, slope, turned_ref, block, width):
    signal = (slope * value).astype(BF).astype(F32)
    return value + STEP * adjoint_conv(signal, turned_ref, block, width)


def relaxed(right, slope_ref, turned_ref, width):
    for block in range(turned_ref.shape[0] - 1, -1, -1):
        right = block_map(right, slope_ref[block], turned_ref, block, width)
    return right


def load_body(width, points_far, terminal_far, states_far, kernels_far, rough_ref, points_ref, states_ref, kernels_ref, edge_ref, sems):
    held = [
        pltpu.make_async_copy(points_far, points_ref, sems.at[0]),
        pltpu.make_async_copy(kernels_far, kernels_ref, sems.at[1]),
        pltpu.make_async_copy(states_far, states_ref, sems.at[2]),
    ]
    for copy in held:
        copy.start()
    edge = Edge(terminal_far, edge_ref, sems.at[3])
    held[0].wait()
    edge.write(points_ref, rough_ref)
    held[1].wait()
    held[2].wait()


def slope_body(width, states_ref, kernels_ref, slope_ref, turned_ref):
    blocks, _, height, _, channels = states_ref.shape
    for block in range(blocks):
        value = states_ref[block, 0].reshape(height * width, channels).astype(F32)
        patches = jnp.concatenate(forward_patches(value, width), 1)
        taps = kernels_ref[block].reshape(9 * channels, channels)
        act = jnp.tanh(jnp.dot(patches, taps, preferred_element_type=F32))
        slope_ref[block] = (1.0 - act * act).astype(BF)
        for i in range(3):
            for j in range(3):
                at = (i * 3 + j) * channels
                turned_ref[block, at : at + channels, :] = kernels_ref[block, i, j].T


def entering(swapped_ref, shifted_ref):
    return jnp.where(is_even(), swapped_ref[...], shifted_ref[...]).astype(F32)


class Edge:
    def __init__(self, terminal_far, edge_ref, sem):
        self.copy = pltpu.make_async_copy(terminal_far, edge_ref, sem)
        self.edge_ref = edge_ref
        pl.when(is_first())(self.copy.start)

    def write(self, points_ref, send_ref):
        @pl.when(is_first())
        def _():
            self.copy.wait()
            send_ref[...] = self.edge_ref[...].astype(BF)

        @pl.when(jnp.logical_not(is_first()))
        def _():
            send_ref[...] = points_ref[...].astype(BF)


def sweep(right, slope_ref, turned_ref, points_ref, width):
    points = points_ref[...]
    points_ref[...] = points + DAMPING * (relaxed(right, slope_ref, turned_ref, width) - points)


def even_body(width, swapped_ref, terminal_far, slope_ref, turned_ref, _, points_ref, send_ref, edge_ref, sem):
    edge = Edge(terminal_far, edge_ref, sem)

    @pl.when(is_even())
    def _():
        sweep(swapped_ref[...].astype(F32), slope_ref, turned_ref, points_ref, width)

    edge.write(points_ref, send_ref)


def odd_body(width, shifted_ref, slope_ref, turned_ref, _, points_ref, send_ref):
    @pl.when(jnp.logical_not(is_even()))
    def _():
        sweep(shifted_ref[...].astype(F32), slope_ref, turned_ref, points_ref, width)

    send_ref[...] = points_ref[...].astype(BF)


def sweep_body(width, swapped_ref, shifted_ref, terminal_far, slope_ref, turned_ref, _, points_ref, send_ref, edge_ref, sem):
    edge = Edge(terminal_far, edge_ref, sem)
    sweep(entering(swapped_ref, shifted_ref), slope_ref, turned_ref, points_ref, width)
    edge.write(points_ref, send_ref)


def residual_body(width, shifted_ref, slope_ref, turned_ref, _, gain_far, relax_far, send_far, points_ref, gain_ref, relax_ref, send_ref, sems):
    gain_copy = pltpu.make_async_copy(gain_far, gain_ref, sems.at[0])
    gain_copy.start()
    relax_copy = pltpu.make_async_copy(relax_ref, relax_far, sems.at[2])

    @stage
    def _():
        relax_ref[...] = relaxed(shifted_ref[...].astype(F32), slope_ref, turned_ref, width)

    @stage
    def _():
        gain_copy.wait()
        residual = (relax_ref[...] - points_ref[...]).reshape(32, 8, 256)
        decay = (1.0 - gain_ref[...]).reshape(32, 8, 256)
        for half in range(2):
            lanes = slice(128 * half, 128 * half + 128)
            send_ref[:, half] = jnp.concatenate([residual[:, :, lanes], decay[:, :, lanes]], 1).astype(BF)
        send_copy = pltpu.make_async_copy(send_ref, send_far, sems.at[1])
        send_copy.start()
        relax_copy.start()
        points_ref[...] = shifted_ref[...].astype(F32)
        send_copy.wait()
        relax_copy.wait()


def scan_body(given_ref, out_far, out_ref, sem):
    count = given_ref.shape[0]
    error = jnp.zeros((8, 128), F32)
    for at in range(count - 1, -1, -1):
        out_ref[at] = error.astype(BF)
        term = given_ref[at].astype(F32)
        error = error - term[8:] * error + term[:8]
    copy = pltpu.make_async_copy(out_ref, out_far, sem)
    copy.start()
    copy.wait()


def final_body(width, points_ref, error_ref, slope_ref, turned_ref, inner_ref, error_out_ref, signal_ref):
    error = error_ref[...].astype(F32).reshape(32, 2, 8, 128)
    error = jnp.concatenate([error[:, 0], error[:, 1]], 2).reshape(256, 256)
    error_out_ref[...] = error
    right = points_ref[...] + error
    last = (slope_ref[1] * right).astype(BF).astype(F32)
    inner = right + STEP * adjoint_conv(last, turned_ref, 1, width)
    inner_ref[...] = inner
    first = (slope_ref[0] * inner).astype(BF).astype(F32)
    low = lax.broadcasted_iota(jnp.int32, (128, 128), 1) < 64
    for block, signal in ((0, first), (1, last)):
        for half in range(2):
            top = signal[:128, 128 * half : 128 * half + 128]
            bottom = signal[128:, 128 * half : 128 * half + 128]
            signal_ref[2 * half, block] = jnp.where(low, top, pltpu.roll(bottom, 64, 1)).astype(BF)
            signal_ref[2 * half + 1, block] = jnp.where(low, pltpu.roll(top, 64, 1), bottom).astype(BF)


def corrected_body(error_ref, gain_ref, relax_ref, inner_ref, adjoint_far, out_ref, sems):
    inner_copy = pltpu.make_async_copy(inner_ref, adjoint_far.at[1], sems.at[1])
    inner_copy.start()
    out_ref[...] = gain_ref[...] * error_ref[...] + relax_ref[...]
    out_copy = pltpu.make_async_copy(out_ref, adjoint_far.at[0], sems.at[0])
    out_copy.start()
    inner_copy.wait()
    out_copy.wait()


def turn_body(*refs):
    out_ref = refs[-1]
    for image, states_ref in enumerate(refs[:-1]):
        for block in range(states_ref.shape[0]):
            out_ref[block, :, 256 * image : 256 * image + 256] = states_ref[block].T


def taps_body(width, *refs, images):
    states_ref, signal_refs = refs[0], refs[1 : 1 + images]
    out_far, out_ref, sems = refs[1 + images :]
    low = lax.broadcasted_iota(jnp.int32, (128, 128), 1) < 64
    wide = lax.broadcasted_iota(jnp.int32, (256, 128), 1) < 64
    copies = [
        pltpu.make_async_copy(out_ref.at[block], out_far.at[block], sems.at[block])
        for block in range(out_ref.shape[0])
    ]

    def one(block):
        parts = []
        for image in range(images):
            packed = signal_refs[image][block].astype(F32)
            other = pltpu.roll(packed, 64, 1)
            both = jnp.concatenate([jnp.where(low, packed, other), jnp.where(low, other, packed)], 0)
            patches = adjoint_patches(both, width)
            patches.append(patches[-1])
            parts.append(
                jnp.concatenate([jnp.where(wide, patches[2 * k], patches[2 * k + 1]) for k in range(5)], 1)
            )
        moved = jnp.concatenate(parts, 0)
        grads = (STEP * jnp.dot(states_ref[block], moved, preferred_element_type=F32)).T
        for tap in range(9):
            out_ref[block, tap // 3, tap % 3] = grads[64 * tap : 64 * tap + 64]
        copies[block].start()

    for block in range(out_ref.shape[0]):
        stage(functools.partial(one, block))
    for copy in copies:
        copy.wait()


def on_device(states, kernels, adjoint_guess, coarse_gain, terminal):
    blocks, _, height, width, channels = states.shape
    cells = height * width
    slabs = lax.axis_size("layer")
    images = lax.axis_size("dp")
    places = [1, 3, 2] if images == 4 else list(range(1, images))
    here = lax.axis_index("dp")
    slab = lax.axis_index("layer")
    conv_flops = 2 * cells * 9 * channels * channels
    shape = jax.ShapeDtypeStruct

    def swapped(part):
        return lax.ppermute(part, "layer", [(i ^ 1, i) for i in range(slabs)])

    def shifted(part):
        return lax.ppermute(part, "layer", [((i + 1) % slabs, i) for i in range(slabs)])

    whole = shape((cells, channels), F32)
    rounded = shape((cells, channels), BF)

    def step(body, outs, *ins, name, **more):
        return call(functools.partial(body, width), outs, ins, flops=blocks * conv_flops, name=name, **more)

    points = adjoint_guess.reshape(cells, channels)
    last_value = terminal.reshape(cells, channels)
    gain = coarse_gain.reshape(cells, channels)
    rough, points, near_states, near_kernels = step(
        load_body,
        (rounded, whole, shape(states.shape, BF), shape(kernels.shape, BF)),
        points,
        last_value,
        states,
        kernels,
        name="load",
        far_in=(0, 1, 2, 3),
        scratch=(pltpu.VMEM((cells, channels), F32), pltpu.SemaphoreType.DMA((4,))),
    )
    across, beside = shifted(rough), swapped(rough)
    slopes, turned = step(
        slope_body,
        (shape((blocks, cells, channels), BF), shape((blocks, 9 * channels, channels), BF)),
        near_states,
        near_kernels,
        name="slopes",
    )
    edge = (pltpu.VMEM((cells, channels), F32), pltpu.SemaphoreType.DMA)
    points, send = step(
        even_body,
        (whole, rounded),
        beside,
        last_value,
        slopes,
        turned,
        points,
        name="even",
        alias={4: 0},
        far_in=(1,),
        scratch=edge,
    )
    next_across = shifted(send)
    points, send = step(
        odd_body, (whole, rounded), across, slopes, turned, points, name="odd", alias={3: 0}
    )
    across = jnp.where(slab == slabs, jnp.zeros_like(next_across), next_across)
    points, send = step(
        sweep_body,
        (whole, rounded),
        swapped(send),
        across,
        last_value,
        slopes,
        turned,
        points,
        name="sweep",
        alias={5: 0},
        far_in=(2,),
        scratch=edge,
    )
    across = shifted(send)
    packed = (32, 2, 16, 128)
    relax, send, points = step(
        residual_body,
        (whole, shape(packed, BF), whole),
        across,
        slopes,
        turned,
        points,
        gain,
        name="residual",
        far_in=(4,),
        far_out=(0, 1),
        alias={3: 2},
        scratch=(
            pltpu.VMEM((cells, channels), F32),
            pltpu.VMEM((cells, channels), F32),
            pltpu.VMEM(packed, BF),
            pltpu.SemaphoreType.DMA((3,)),
        ),
    )

    def spread(parts):
        return lax.all_to_all(parts, "layer", 0, 0, tiled=True)

    own_states, send = lax.optimization_barrier((states.reshape(blocks, cells, channels), send))
    errors = call(
        scan_body,
        shape((slabs, 8, 128), BF),
        (spread(send.reshape(slabs, 16, 128)),),
        name="scan",
        moved=0,
        far_out=(0,),
        scratch=(pltpu.VMEM((slabs, 8, 128), BF), pltpu.SemaphoreType.DMA),
    )
    error = spread(errors)
    all_states = [own_states]
    for k in places:
        all_states.append(lax.ppermute(own_states, "dp", [(i, (i + k) % images) for i in range(images)]))
    states_turned = call(
        turn_body, shape((blocks, channels, images * cells), BF), all_states, name="turn"
    )
    error, states_turned = lax.optimization_barrier((error, states_turned))
    inner, error, signals = step(
        final_body,
        (whole, whole, shape((images, blocks, 128, 128), BF)),
        points,
        error,
        slopes,
        turned,
        name="final",
    )

    received = [lax.dynamic_index_in_dim(signals, here, 0, keepdims=False)]
    for k in places:
        part = lax.dynamic_index_in_dim(signals, (here + k) % images, 0, keepdims=False)
        received.append(lax.ppermute(part, "dp", [(i, (i + k) % images) for i in range(images)]))
    adjoint = call(
        corrected_body, shape((blocks, cells, channels), F32), (error, gain, relax, inner), name="corrected", far_out=(0,),
        scratch=(pltpu.VMEM((cells, channels), F32), pltpu.SemaphoreType.DMA((2,))),
    )
    slices = (blocks, 3, 3, channels // images, channels)
    grads = step(
        functools.partial(taps_body, images=images),
        shape(slices, F32),
        states_turned,
        *received,
        name="taps",
        far_out=(0,),
        scratch=(pltpu.VMEM(slices, F32), pltpu.SemaphoreType.DMA((blocks,))),
    )
    return adjoint.reshape(blocks, 1, height, width, channels), jnp.swapaxes(grads, 3, 4)


def solution(mesh):
    in_specs = (
        P("layer", "dp", None, None, None),
        P("layer", None, None, None, None),
        P("layer", "dp", None, None, None),
        P("layer", None, None, None),
        P("dp", None, None, None),
    )
    out_specs = (P("layer", "dp", None, None, None), P("layer", None, None, None, "dp"))
    return jax.shard_map(
        on_device, mesh=mesh, in_specs=in_specs, out_specs=out_specs, check_vma=False
    )
```

```python
import functools

import jax
import jax.numpy as jnp
from jax import lax
from jax.experimental import pallas as pl
from jax.experimental.pallas import tpu as pltpu
from jax.sharding import PartitionSpec as P

STEP = 0.5
DAMPING = 0.5
BF = jnp.bfloat16
F32 = jnp.float32
VMEM_LIMIT = 12 * 1024 * 1024


def call(body, outs, ins, flops=0, moved=2_000_000, name=None, scratch=(), far_in=(), far_out=(), alias=None):
    def spec(far):
        return pl.BlockSpec(memory_space=pltpu.HBM if far else pltpu.VMEM)

    single = not isinstance(outs, tuple)
    placed = tuple(
        (pltpu.HBM if k in far_out else pltpu.VMEM)(out.shape, out.dtype)
        for k, out in enumerate((outs,) if single else outs)
    )
    ins = [
        pltpu.with_memory_space_constraint(value, pltpu.HBM if k in far_in else pltpu.VMEM)
        for k, value in enumerate(ins)
    ]
    out_specs = [spec(k in far_out) for k in range(1 if single else len(outs))]
    return pl.pallas_call(
        body,
        out_shape=placed[0] if single else placed,
        in_specs=[spec(k in far_in) for k in range(len(ins))],
        out_specs=out_specs[0] if single else tuple(out_specs),
        scratch_shapes=scratch,
        input_output_aliases=alias or {},
        compiler_params=pltpu.CompilerParams(vmem_limit_bytes=VMEM_LIMIT),
        cost_estimate=pl.CostEstimate(flops=flops, bytes_accessed=moved, transcendentals=0),
        name=name,
    )(*ins)


def is_even():
    return lax.axis_index("layer") % 2 == 0


def stage(body):
    pl.when(lax.axis_index("layer") >= 0)(body)


def is_first():
    return lax.axis_index("layer") == 0


def columns(value, width):
    cells = value.shape[0]
    col = lax.broadcasted_iota(jnp.int32, value.shape, 0) % width
    ahead = jnp.where(col == width - 1, 0.0, pltpu.roll(value, cells - 1, 0))
    behind = jnp.where(col == 0, 0.0, pltpu.roll(value, 1, 0))
    return ahead, value, behind


def rows(value, width):
    edge = jnp.zeros((width, value.shape[1]), value.dtype)
    return jnp.concatenate([edge, value, edge], 0)


def forward_patches(value, width):
    cells = value.shape[0]
    ahead, here, behind = columns(value, width)
    padded = [rows(part.astype(BF), width) for part in (behind, here, ahead)]
    return [padded[j][i * width : i * width + cells] for i in range(3) for j in range(3)]


def adjoint_patches(value, width):
    cells = value.shape[0]
    ahead, here, behind = columns(value, width)
    padded = [rows(part.astype(BF), width) for part in (ahead, here, behind)]
    return [padded[j][(2 - i) * width : (2 - i) * width + cells] for i in range(3) for j in range(3)]


def adjoint_conv(signal, turned_ref, block, width):
    patches = jnp.concatenate(adjoint_patches(signal, width), 1)
    return jnp.dot(patches, turned_ref[block], preferred_element_type=F32)


def block_map(value, slope, turned_ref, block, width):
    signal = (slope * value).astype(BF).astype(F32)
    return value + STEP * adjoint_conv(signal, turned_ref, block, width)


def relaxed(right, slope_ref, turned_ref, width):
    for block in range(turned_ref.shape[0] - 1, -1, -1):
        right = block_map(right, slope_ref[block], turned_ref, block, width)
    return right


def load_body(width, points_far, terminal_far, states_far, kernels_far, rough_ref, points_ref, states_ref, kernels_ref, edge_ref, sems):
    held = [
        pltpu.make_async_copy(points_far, points_ref, sems.at[0]),
        pltpu.make_async_copy(kernels_far, kernels_ref, sems.at[1]),
        pltpu.make_async_copy(states_far, states_ref, sems.at[2]),
    ]
    for copy in held:
        copy.start()
    edge = Edge(terminal_far, edge_ref, sems.at[3])
    held[0].wait()
    edge.write(points_ref, rough_ref)
    held[1].wait()
    held[2].wait()


def slope_body(width, states_ref, kernels_ref, slope_ref, turned_ref):
    blocks, _, height, _, channels = states_ref.shape
    for block in range(blocks):
        value = states_ref[block, 0].reshape(height * width, channels).astype(F32)
        patches = jnp.concatenate(forward_patches(value, width), 1)
        taps = kernels_ref[block].reshape(9 * channels, channels)
        act = jnp.tanh(jnp.dot(patches, taps, preferred_element_type=F32))
        slope_ref[block] = (1.0 - act * act).astype(BF)
        for i in range(3):
            for j in range(3):
                at = (i * 3 + j) * channels
                turned_ref[block, at : at + channels, :] = kernels_ref[block, i, j].T


def entering(swapped_ref, shifted_ref):
    return jnp.where(is_even(), swapped_ref[...], shifted_ref[...]).astype(F32)


class Edge:
    def __init__(self, terminal_far, edge_ref, sem):
        self.copy = pltpu.make_async_copy(terminal_far, edge_ref, sem)
        self.edge_ref = edge_ref
        pl.when(is_first())(self.copy.start)

    def write(self, points_ref, send_ref):
        @pl.when(is_first())
        def _():
            self.copy.wait()
            send_ref[...] = self.edge_ref[...].astype(BF)

        @pl.when(jnp.logical_not(is_first()))
        def _():
            send_ref[...] = points_ref[...].astype(BF)


def sweep(right, slope_ref, turned_ref, points_ref, width):
    points = points_ref[...]
    points_ref[...] = points + DAMPING * (relaxed(right, slope_ref, turned_ref, width) - points)


def even_body(width, swapped_ref, terminal_far, slope_ref, turned_ref, _, points_ref, send_ref, edge_ref, sem):
    edge = Edge(terminal_far, edge_ref, sem)

    @pl.when(is_even())
    def _():
        sweep(swapped_ref[...].astype(F32), slope_ref, turned_ref, points_ref, width)

    edge.write(points_ref, send_ref)


def odd_body(width, shifted_ref, slope_ref, turned_ref, _, points_ref, send_ref):
    @pl.when(jnp.logical_not(is_even()))
    def _():
        sweep(shifted_ref[...].astype(F32), slope_ref, turned_ref, points_ref, width)

    send_ref[...] = points_ref[...].astype(BF)


def sweep_body(width, swapped_ref, shifted_ref, terminal_far, slope_ref, turned_ref, _, points_ref, send_ref, edge_ref, sem):
    edge = Edge(terminal_far, edge_ref, sem)
    sweep(entering(swapped_ref, shifted_ref), slope_ref, turned_ref, points_ref, width)
    edge.write(points_ref, send_ref)


def residual_body(width, shifted_ref, slope_ref, turned_ref, _, gain_far, relax_far, send_far, points_ref, gain_ref, relax_ref, send_ref, sems):
    gain_copy = pltpu.make_async_copy(gain_far, gain_ref, sems.at[0])
    gain_copy.start()
    relax_copy = pltpu.make_async_copy(relax_ref, relax_far, sems.at[2])

    @stage
    def _():
        relax_ref[...] = relaxed(shifted_ref[...].astype(F32), slope_ref, turned_ref, width)

    @stage
    def _():
        gain_copy.wait()
        residual = (relax_ref[...] - points_ref[...]).reshape(32, 8, 256)
        decay = (1.0 - gain_ref[...]).reshape(32, 8, 256)
        for half in range(2):
            lanes = slice(128 * half, 128 * half + 128)
            send_ref[:, half] = jnp.concatenate([residual[:, :, lanes], decay[:, :, lanes]], 1).astype(BF)
        send_copy = pltpu.make_async_copy(send_ref, send_far, sems.at[1])
        send_copy.start()
        relax_copy.start()
        points_ref[...] = shifted_ref[...].astype(F32)
        send_copy.wait()
        relax_copy.wait()


def scan_body(given_ref, out_far, out_ref, sem):
    count = given_ref.shape[0]
    error = jnp.zeros((8, 128), F32)
    for at in range(count - 1, -1, -1):
        out_ref[at] = error.astype(BF)
        term = given_ref[at].astype(F32)
        error = error - term[8:] * error + term[:8]
    copy = pltpu.make_async_copy(out_ref, out_far, sem)
    copy.start()
    copy.wait()


def final_body(width, points_ref, error_ref, slope_ref, turned_ref, inner_ref, error_out_ref, signal_ref):
    error = error_ref[...].astype(F32).reshape(32, 2, 8, 128)
    error = jnp.concatenate([error[:, 0], error[:, 1]], 2).reshape(256, 256)
    error_out_ref[...] = error
    right = points_ref[...] + error
    last = (slope_ref[1] * right).astype(BF).astype(F32)
    inner = right + STEP * adjoint_conv(last, turned_ref, 1, width)
    inner_ref[...] = inner
    first = (slope_ref[0] * inner).astype(BF).astype(F32)
    low = lax.broadcasted_iota(jnp.int32, (128, 128), 1) < 64
    for block, signal in ((0, first), (1, last)):
        for half in range(2):
            top = signal[:128, 128 * half : 128 * half + 128]
            bottom = signal[128:, 128 * half : 128 * half + 128]
            signal_ref[2 * half, block] = jnp.where(low, top, pltpu.roll(bottom, 64, 1)).astype(BF)
            signal_ref[2 * half + 1, block] = jnp.where(low, pltpu.roll(top, 64, 1), bottom).astype(BF)


def corrected_body(error_ref, gain_ref, relax_ref, inner_ref, adjoint_far, out_ref, sems):
    inner_copy = pltpu.make_async_copy(inner_ref, adjoint_far.at[1], sems.at[1])
    inner_copy.start()
    out_ref[...] = gain_ref[...] * error_ref[...] + relax_ref[...]
    out_copy = pltpu.make_async_copy(out_ref, adjoint_far.at[0], sems.at[0])
    out_copy.start()
    inner_copy.wait()
    out_copy.wait()


def turn_body(*refs):
    out_ref = refs[-1]
    for image, states_ref in enumerate(refs[:-1]):
        for block in range(states_ref.shape[0]):
            out_ref[block, :, 256 * image : 256 * image + 256] = states_ref[block].T


def taps_body(width, *refs, images):
    states_ref, signal_refs = refs[0], refs[1 : 1 + images]
    out_far, out_ref, sems = refs[1 + images :]
    low = lax.broadcasted_iota(jnp.int32, (128, 128), 1) < 64
    wide = lax.broadcasted_iota(jnp.int32, (256, 128), 1) < 64
    copies = [
        pltpu.make_async_copy(out_ref.at[block], out_far.at[block], sems.at[block])
        for block in range(out_ref.shape[0])
    ]

    def one(block):
        parts = []
        for image in range(images):
            packed = signal_refs[image][block].astype(F32)
            other = pltpu.roll(packed, 64, 1)
            both = jnp.concatenate([jnp.where(low, packed, other), jnp.where(low, other, packed)], 0)
            patches = adjoint_patches(both, width)
            patches.append(patches[-1])
            parts.append(
                jnp.concatenate([jnp.where(wide, patches[2 * k], patches[2 * k + 1]) for k in range(5)], 1)
            )
        moved = jnp.concatenate(parts, 0)
        grads = (STEP * jnp.dot(states_ref[block], moved, preferred_element_type=F32)).T
        for tap in range(9):
            out_ref[block, tap // 3, tap % 3] = grads[64 * tap : 64 * tap + 64]
        copies[block].start()

    for block in range(out_ref.shape[0]):
        stage(functools.partial(one, block))
    for copy in copies:
        copy.wait()


def on_device(states, kernels, adjoint_guess, coarse_gain, terminal):
    blocks, _, height, width, channels = states.shape
    cells = height * width
    slabs = lax.axis_size("layer")
    images = lax.axis_size("dp")
    places = [2, 3, 1] if images == 4 else list(range(1, images))
    here = lax.axis_index("dp")
    slab = lax.axis_index("layer")
    conv_flops = 2 * cells * 9 * channels * channels
    shape = jax.ShapeDtypeStruct

    def swapped(part):
        return lax.ppermute(part, "layer", [(i ^ 1, i) for i in range(slabs)])

    def shifted(part):
        return lax.ppermute(part, "layer", [((i + 1) % slabs, i) for i in range(slabs)])

    whole = shape((cells, channels), F32)
    rounded = shape((cells, channels), BF)

    def step(body, outs, *ins, name, **more):
        return call(functools.partial(body, width), outs, ins, flops=blocks * conv_flops, name=name, **more)

    points = adjoint_guess.reshape(cells, channels)
    last_value = terminal.reshape(cells, channels)
    gain = coarse_gain.reshape(cells, channels)
    rough, points, near_states, near_kernels = step(
        load_body,
        (rounded, whole, shape(states.shape, BF), shape(kernels.shape, BF)),
        points,
        last_value,
        states,
        kernels,
        name="load",
        far_in=(0, 1, 2, 3),
        scratch=(pltpu.VMEM((cells, channels), F32), pltpu.SemaphoreType.DMA((4,))),
    )
    across, beside = shifted(rough), swapped(rough)
    slopes, turned = step(
        slope_body,
        (shape((blocks, cells, channels), BF), shape((blocks, 9 * channels, channels), BF)),
        near_states,
        near_kernels,
        name="slopes",
    )
    edge = (pltpu.VMEM((cells, channels), F32), pltpu.SemaphoreType.DMA)
    points, send = step(
        even_body,
        (whole, rounded),
        beside,
        last_value,
        slopes,
        turned,
        points,
        name="even",
        alias={4: 0},
        far_in=(1,),
        scratch=edge,
    )
    next_across = shifted(send)
    points, send = step(
        odd_body, (whole, rounded), across, slopes, turned, points, name="odd", alias={3: 0}
    )
    across = jnp.where(slab == slabs, jnp.zeros_like(next_across), next_across)
    points, send = step(
        sweep_body,
        (whole, rounded),
        swapped(send),
        across,
        last_value,
        slopes,
        turned,
        points,
        name="sweep",
        alias={5: 0},
        far_in=(2,),
        scratch=edge,
    )
    across = shifted(send)
    packed = (32, 2, 16, 128)
    relax, send, points = step(
        residual_body,
        (whole, shape(packed, BF), whole),
        across,
        slopes,
        turned,
        points,
        gain,
        name="residual",
        far_in=(4,),
        far_out=(0, 1),
        alias={3: 2},
        scratch=(
            pltpu.VMEM((cells, channels), F32),
            pltpu.VMEM((cells, channels), F32),
            pltpu.VMEM(packed, BF),
            pltpu.SemaphoreType.DMA((3,)),
        ),
    )

    def spread(parts):
        return lax.all_to_all(parts, "layer", 0, 0, tiled=True)

    own_states, send = lax.optimization_barrier((states.reshape(blocks, cells, channels), send))
    errors = call(
        scan_body,
        shape((slabs, 8, 128), BF),
        (spread(send.reshape(slabs, 16, 128)),),
        name="scan",
        moved=0,
        far_out=(0,),
        scratch=(pltpu.VMEM((slabs, 8, 128), BF), pltpu.SemaphoreType.DMA),
    )
    error = spread(errors)
    all_states = [own_states]
    for k in places:
        all_states.append(lax.ppermute(own_states, "dp", [(i, (i + k) % images) for i in range(images)]))
    states_turned = call(
        turn_body, shape((blocks, channels, images * cells), BF), all_states, name="turn"
    )
    error, states_turned = lax.optimization_barrier((error, states_turned))
    inner, error, signals = step(
        final_body,
        (whole, whole, shape((images, blocks, 128, 128), BF)),
        points,
        error,
        slopes,
        turned,
        name="final",
    )

    received = [lax.dynamic_index_in_dim(signals, here, 0, keepdims=False)]
    for k in places:
        part = lax.dynamic_index_in_dim(signals, (here + k) % images, 0, keepdims=False)
        received.append(lax.ppermute(part, "dp", [(i, (i + k) % images) for i in range(images)]))
    adjoint = call(
        corrected_body, shape((blocks, cells, channels), F32), (error, gain, relax, inner), name="corrected", far_out=(0,),
        scratch=(pltpu.VMEM((cells, channels), F32), pltpu.SemaphoreType.DMA((2,))),
    )
    slices = (blocks, 3, 3, channels // images, channels)
    grads = step(
        functools.partial(taps_body, images=images),
        shape(slices, F32),
        states_turned,
        *received,
        name="taps",
        far_out=(0,),
        scratch=(pltpu.VMEM(slices, F32), pltpu.SemaphoreType.DMA((blocks,))),
    )
    return adjoint.reshape(blocks, 1, height, width, channels), jnp.swapaxes(grads, 3, 4)


def solution(mesh):
    in_specs = (
        P("layer", "dp", None, None, None),
        P("layer", None, None, None, None),
        P("layer", "dp", None, None, None),
        P("layer", None, None, None),
        P("dp", None, None, None),
    )
    out_specs = (P("layer", "dp", None, None, None), P("layer", None, None, None, "dp"))
    return jax.shard_map(
        on_device, mesh=mesh, in_specs=in_specs, out_specs=out_specs, check_vma=False
    )
```

```python
import functools

import jax
import jax.numpy as jnp
from jax import lax
from jax.experimental import pallas as pl
from jax.experimental.pallas import tpu as pltpu
from jax.sharding import PartitionSpec as P

STEP = 0.5
DAMPING = 0.5
BF = jnp.bfloat16
F32 = jnp.float32
VMEM_LIMIT = 12 * 1024 * 1024


def call(body, outs, ins, flops=0, moved=2_000_000, name=None, scratch=(), far_in=(), far_out=(), alias=None):
    def spec(far):
        return pl.BlockSpec(memory_space=pltpu.HBM if far else pltpu.VMEM)

    single = not isinstance(outs, tuple)
    placed = tuple(
        (pltpu.HBM if k in far_out else pltpu.VMEM)(out.shape, out.dtype)
        for k, out in enumerate((outs,) if single else outs)
    )
    ins = [
        pltpu.with_memory_space_constraint(value, pltpu.HBM if k in far_in else pltpu.VMEM)
        for k, value in enumerate(ins)
    ]
    out_specs = [spec(k in far_out) for k in range(1 if single else len(outs))]
    return pl.pallas_call(
        body,
        out_shape=placed[0] if single else placed,
        in_specs=[spec(k in far_in) for k in range(len(ins))],
        out_specs=out_specs[0] if single else tuple(out_specs),
        scratch_shapes=scratch,
        input_output_aliases=alias or {},
        compiler_params=pltpu.CompilerParams(vmem_limit_bytes=VMEM_LIMIT),
        cost_estimate=pl.CostEstimate(flops=flops, bytes_accessed=moved, transcendentals=0),
        name=name,
    )(*ins)


def is_even():
    return lax.axis_index("layer") % 2 == 0


def stage(body):
    pl.when(lax.axis_index("layer") >= 0)(body)


def is_first():
    return lax.axis_index("layer") == 0


def columns(value, width):
    cells = value.shape[0]
    col = lax.broadcasted_iota(jnp.int32, value.shape, 0) % width
    ahead = jnp.where(col == width - 1, 0.0, pltpu.roll(value, cells - 1, 0))
    behind = jnp.where(col == 0, 0.0, pltpu.roll(value, 1, 0))
    return ahead, value, behind


def rows(value, width):
    edge = jnp.zeros((width, value.shape[1]), value.dtype)
    return jnp.concatenate([edge, value, edge], 0)


def forward_patches(value, width):
    cells = value.shape[0]
    ahead, here, behind = columns(value, width)
    padded = [rows(part.astype(BF), width) for part in (behind, here, ahead)]
    return [padded[j][i * width : i * width + cells] for i in range(3) for j in range(3)]


def adjoint_patches(value, width):
    cells = value.shape[0]
    ahead, here, behind = columns(value, width)
    padded = [rows(part.astype(BF), width) for part in (ahead, here, behind)]
    return [padded[j][(2 - i) * width : (2 - i) * width + cells] for i in range(3) for j in range(3)]


def adjoint_conv(signal, turned_ref, block, width):
    patches = jnp.concatenate(adjoint_patches(signal, width), 1)
    return jnp.dot(patches, turned_ref[block], preferred_element_type=F32)


def block_map(value, slope, turned_ref, block, width):
    signal = (slope * value).astype(BF).astype(F32)
    return value + STEP * adjoint_conv(signal, turned_ref, block, width)


def relaxed(right, slope_ref, turned_ref, width):
    for block in range(turned_ref.shape[0] - 1, -1, -1):
        right = block_map(right, slope_ref[block], turned_ref, block, width)
    return right


def load_body(width, points_far, terminal_far, states_far, kernels_far, rough_ref, points_ref, states_ref, kernels_ref, edge_ref, sems):
    held = [
        pltpu.make_async_copy(points_far, points_ref, sems.at[0]),
        pltpu.make_async_copy(kernels_far, kernels_ref, sems.at[1]),
        pltpu.make_async_copy(states_far, states_ref, sems.at[2]),
    ]
    for copy in held:
        copy.start()
    edge = Edge(terminal_far, edge_ref, sems.at[3])
    held[0].wait()
    edge.write(points_ref, rough_ref)
    held[1].wait()
    held[2].wait()


def slope_body(width, states_ref, kernels_ref, slope_ref, turned_ref):
    blocks, _, height, _, channels = states_ref.shape
    for block in range(blocks):
        value = states_ref[block, 0].reshape(height * width, channels).astype(F32)
        patches = jnp.concatenate(forward_patches(value, width), 1)
        taps = kernels_ref[block].reshape(9 * channels, channels)
        act = jnp.tanh(jnp.dot(patches, taps, preferred_element_type=F32))
        slope_ref[block] = (1.0 - act * act).astype(BF)
        for i in range(3):
            for j in range(3):
                at = (i * 3 + j) * channels
                turned_ref[block, at : at + channels, :] = kernels_ref[block, i, j].T


def entering(swapped_ref, shifted_ref):
    return jnp.where(is_even(), swapped_ref[...], shifted_ref[...]).astype(F32)


class Edge:
    def __init__(self, terminal_far, edge_ref, sem):
        self.copy = pltpu.make_async_copy(terminal_far, edge_ref, sem)
        self.edge_ref = edge_ref
        pl.when(is_first())(self.copy.start)

    def write(self, points_ref, send_ref):
        @pl.when(is_first())
        def _():
            self.copy.wait()
            send_ref[...] = self.edge_ref[...].astype(BF)

        @pl.when(jnp.logical_not(is_first()))
        def _():
            send_ref[...] = points_ref[...].astype(BF)


def sweep(right, slope_ref, turned_ref, points_ref, width):
    points = points_ref[...]
    points_ref[...] = points + DAMPING * (relaxed(right, slope_ref, turned_ref, width) - points)


def even_body(width, swapped_ref, terminal_far, slope_ref, turned_ref, _, points_ref, send_ref, edge_ref, sem):
    edge = Edge(terminal_far, edge_ref, sem)

    @pl.when(is_even())
    def _():
        sweep(swapped_ref[...].astype(F32), slope_ref, turned_ref, points_ref, width)

    edge.write(points_ref, send_ref)


def odd_body(width, shifted_ref, slope_ref, turned_ref, _, points_ref, send_ref):
    @pl.when(jnp.logical_not(is_even()))
    def _():
        sweep(shifted_ref[...].astype(F32), slope_ref, turned_ref, points_ref, width)

    send_ref[...] = points_ref[...].astype(BF)


def sweep_body(width, swapped_ref, shifted_ref, terminal_far, slope_ref, turned_ref, _, points_ref, send_ref, edge_ref, sem):
    edge = Edge(terminal_far, edge_ref, sem)
    sweep(entering(swapped_ref, shifted_ref), slope_ref, turned_ref, points_ref, width)
    edge.write(points_ref, send_ref)


def residual_body(width, shifted_ref, slope_ref, turned_ref, _, gain_far, relax_far, send_far, points_ref, gain_ref, relax_ref, send_ref, sems):
    gain_copy = pltpu.make_async_copy(gain_far, gain_ref, sems.at[0])
    gain_copy.start()
    relax_copy = pltpu.make_async_copy(relax_ref, relax_far, sems.at[2])

    @stage
    def _():
        relax_ref[...] = relaxed(shifted_ref[...].astype(F32), slope_ref, turned_ref, width)

    @stage
    def _():
        gain_copy.wait()
        residual = (relax_ref[...] - points_ref[...]).reshape(32, 8, 256)
        decay = (1.0 - gain_ref[...]).reshape(32, 8, 256)
        for half in range(2):
            lanes = slice(128 * half, 128 * half + 128)
            send_ref[:, half] = jnp.concatenate([residual[:, :, lanes], decay[:, :, lanes]], 1).astype(BF)
        send_copy = pltpu.make_async_copy(send_ref, send_far, sems.at[1])
        send_copy.start()
        relax_copy.start()
        points_ref[...] = shifted_ref[...].astype(F32)
        send_copy.wait()
        relax_copy.wait()


def scan_body(given_ref, out_far, out_ref, carry_ref, sems):
    count = given_ref.shape[0]
    half = count // 2
    parts = [pl.ds(0, half), pl.ds(half, count - half)]
    copies = [pltpu.make_async_copy(out_ref.at[part], out_far.at[part], sems.at[k]) for k, part in enumerate(parts)]

    def sweep_down(first, stop, error):
        for at in range(first - 1, stop - 1, -1):
            out_ref[at] = error.astype(BF)
            term = given_ref[at].astype(F32)
            error = error - term[8:] * error + term[:8]
        return error

    carry_ref[...] = sweep_down(count, half, jnp.zeros((8, 128), F32))
    copies[1].start()

    @stage
    def _():
        sweep_down(half, 0, carry_ref[...])
        copies[0].start()

    for copy in copies:
        copy.wait()


def final_body(width, points_ref, error_ref, slope_ref, turned_ref, inner_ref, error_out_ref, signal_ref):
    error = error_ref[...].astype(F32).reshape(32, 2, 8, 128)
    error = jnp.concatenate([error[:, 0], error[:, 1]], 2).reshape(256, 256)
    error_out_ref[...] = error
    right = points_ref[...] + error
    last = (slope_ref[1] * right).astype(BF).astype(F32)
    inner = right + STEP * adjoint_conv(last, turned_ref, 1, width)
    inner_ref[...] = inner
    first = (slope_ref[0] * inner).astype(BF).astype(F32)
    low = lax.broadcasted_iota(jnp.int32, (128, 128), 1) < 64
    for block, signal in ((0, first), (1, last)):
        for half in range(2):
            top = signal[:128, 128 * half : 128 * half + 128]
            bottom = signal[128:, 128 * half : 128 * half + 128]
            signal_ref[2 * half, block] = jnp.where(low, top, pltpu.roll(bottom, 64, 1)).astype(BF)
            signal_ref[2 * half + 1, block] = jnp.where(low, pltpu.roll(top, 64, 1), bottom).astype(BF)


def corrected_body(error_ref, gain_ref, relax_ref, inner_ref, adjoint_far, out_ref, sems):
    inner_copy = pltpu.make_async_copy(inner_ref, adjoint_far.at[1], sems.at[1])
    inner_copy.start()
    out_ref[...] = gain_ref[...] * error_ref[...] + relax_ref[...]
    out_copy = pltpu.make_async_copy(out_ref, adjoint_far.at[0], sems.at[0])
    out_copy.start()
    inner_copy.wait()
    out_copy.wait()


def turn_body(*refs):
    out_ref = refs[-1]
    for image, states_ref in enumerate(refs[:-1]):
        for block in range(states_ref.shape[0]):
            out_ref[block, :, 256 * image : 256 * image + 256] = states_ref[block].T


def taps_body(width, *refs, images):
    states_ref, signal_refs = refs[0], refs[1 : 1 + images]
    out_far, out_ref, sems = refs[1 + images :]
    low = lax.broadcasted_iota(jnp.int32, (128, 128), 1) < 64
    wide = lax.broadcasted_iota(jnp.int32, (256, 128), 1) < 64
    copies = [
        pltpu.make_async_copy(out_ref.at[block], out_far.at[block], sems.at[block])
        for block in range(out_ref.shape[0])
    ]

    def one(block):
        parts = []
        for image in range(images):
            packed = signal_refs[image][block].astype(F32)
            other = pltpu.roll(packed, 64, 1)
            both = jnp.concatenate([jnp.where(low, packed, other), jnp.where(low, other, packed)], 0)
            patches = adjoint_patches(both, width)
            patches.append(patches[-1])
            parts.append(
                jnp.concatenate([jnp.where(wide, patches[2 * k], patches[2 * k + 1]) for k in range(5)], 1)
            )
        moved = jnp.concatenate(parts, 0)
        grads = (STEP * jnp.dot(states_ref[block], moved, preferred_element_type=F32)).T
        for tap in range(9):
            out_ref[block, tap // 3, tap % 3] = grads[64 * tap : 64 * tap + 64]
        copies[block].start()

    for block in range(out_ref.shape[0]):
        stage(functools.partial(one, block))
    for copy in copies:
        copy.wait()


def on_device(states, kernels, adjoint_guess, coarse_gain, terminal):
    blocks, _, height, width, channels = states.shape
    cells = height * width
    slabs = lax.axis_size("layer")
    images = lax.axis_size("dp")
    places = [2, 3, 1] if images == 4 else list(range(1, images))
    here = lax.axis_index("dp")
    slab = lax.axis_index("layer")
    conv_flops = 2 * cells * 9 * channels * channels
    shape = jax.ShapeDtypeStruct

    def swapped(part):
        return lax.ppermute(part, "layer", [(i ^ 1, i) for i in range(slabs)])

    def shifted(part):
        return lax.ppermute(part, "layer", [((i + 1) % slabs, i) for i in range(slabs)])

    whole = shape((cells, channels), F32)
    rounded = shape((cells, channels), BF)

    def step(body, outs, *ins, name, **more):
        return call(functools.partial(body, width), outs, ins, flops=blocks * conv_flops, name=name, **more)

    points = adjoint_guess.reshape(cells, channels)
    last_value = terminal.reshape(cells, channels)
    gain = coarse_gain.reshape(cells, channels)
    rough, points, near_states, near_kernels = step(
        load_body,
        (rounded, whole, shape(states.shape, BF), shape(kernels.shape, BF)),
        points,
        last_value,
        states,
        kernels,
        name="load",
        far_in=(0, 1, 2, 3),
        scratch=(pltpu.VMEM((cells, channels), F32), pltpu.SemaphoreType.DMA((4,))),
    )
    across, beside = shifted(rough), swapped(rough)
    slopes, turned = step(
        slope_body,
        (shape((blocks, cells, channels), BF), shape((blocks, 9 * channels, channels), BF)),
        near_states,
        near_kernels,
        name="slopes",
    )
    edge = (pltpu.VMEM((cells, channels), F32), pltpu.SemaphoreType.DMA)
    points, send = step(
        even_body,
        (whole, rounded),
        beside,
        last_value,
        slopes,
        turned,
        points,
        name="even",
        alias={4: 0},
        far_in=(1,),
        scratch=edge,
    )
    next_across = shifted(send)
    points, send = step(
        odd_body, (whole, rounded), across, slopes, turned, points, name="odd", alias={3: 0}
    )
    across = jnp.where(slab == slabs, jnp.zeros_like(next_across), next_across)
    points, send = step(
        sweep_body,
        (whole, rounded),
        swapped(send),
        across,
        last_value,
        slopes,
        turned,
        points,
        name="sweep",
        alias={5: 0},
        far_in=(2,),
        scratch=edge,
    )
    across = shifted(send)
    packed = (32, 2, 16, 128)
    relax, send, points = step(
        residual_body,
        (whole, shape(packed, BF), whole),
        across,
        slopes,
        turned,
        points,
        gain,
        name="residual",
        far_in=(4,),
        far_out=(0, 1),
        alias={3: 2},
        scratch=(
            pltpu.VMEM((cells, channels), F32),
            pltpu.VMEM((cells, channels), F32),
            pltpu.VMEM(packed, BF),
            pltpu.SemaphoreType.DMA((3,)),
        ),
    )

    def spread(parts):
        return lax.all_to_all(parts, "layer", 0, 0, tiled=True)

    own_states, send = lax.optimization_barrier((states.reshape(blocks, cells, channels), send))
    errors = call(
        scan_body,
        shape((slabs, 8, 128), BF),
        (spread(send.reshape(slabs, 16, 128)),),
        name="scan",
        moved=0,
        far_out=(0,),
        scratch=(
            pltpu.VMEM((slabs, 8, 128), BF),
            pltpu.VMEM((8, 128), F32),
            pltpu.SemaphoreType.DMA((2,)),
        ),
    )
    error = spread(errors)
    all_states = [own_states]
    for k in places:
        all_states.append(lax.ppermute(own_states, "dp", [(i, (i + k) % images) for i in range(images)]))
    states_turned = call(
        turn_body, shape((blocks, channels, images * cells), BF), all_states, name="turn"
    )
    error, states_turned = lax.optimization_barrier((error, states_turned))
    inner, error, signals = step(
        final_body,
        (whole, whole, shape((images, blocks, 128, 128), BF)),
        points,
        error,
        slopes,
        turned,
        name="final",
    )

    received = [lax.dynamic_index_in_dim(signals, here, 0, keepdims=False)]
    for k in places:
        part = lax.dynamic_index_in_dim(signals, (here + k) % images, 0, keepdims=False)
        received.append(lax.ppermute(part, "dp", [(i, (i + k) % images) for i in range(images)]))
    adjoint = call(
        corrected_body, shape((blocks, cells, channels), F32), (error, gain, relax, inner), name="corrected", far_out=(0,),
        scratch=(pltpu.VMEM((cells, channels), F32), pltpu.SemaphoreType.DMA((2,))),
    )
    slices = (blocks, 3, 3, channels // images, channels)
    grads = step(
        functools.partial(taps_body, images=images),
        shape(slices, F32),
        states_turned,
        *received,
        name="taps",
        far_out=(0,),
        scratch=(pltpu.VMEM(slices, F32), pltpu.SemaphoreType.DMA((blocks,))),
    )
    return adjoint.reshape(blocks, 1, height, width, channels), jnp.swapaxes(grads, 3, 4)


def solution(mesh):
    in_specs = (
        P("layer", "dp", None, None, None),
        P("layer", None, None, None, None),
        P("layer", "dp", None, None, None),
        P("layer", None, None, None),
        P("dp", None, None, None),
    )
    out_specs = (P("layer", "dp", None, None, None), P("layer", None, None, None, "dp"))
    return jax.shard_map(
        on_device, mesh=mesh, in_specs=in_specs, out_specs=out_specs, check_vma=False
    )
```
